128 devices in a mesh: section: 8 (over x, core), replica: 4 (over y), dp: 4 (over z).
Axes of the slice: x: 4, y: 4, z: 4, core: 2. Of those that a mesh axis runs over, the one named last changes fastest.
Arguments:
- features: bfloat16 [32, 1024, 512], P(('section', 'dp'), 'replica'), may hold values from -6 to 6
- tile_vals: bfloat16 [32, 4, 8, 48, 128, 128], P(('section', 'dp'), 'replica'), may hold values from -0.078125 to 0.078125
- tile_cols: int32 [32, 4, 8, 48], P(('section', 'dp'), 'replica'), may hold values from 0 to 63, as said below
- row_counts: int32 [32, 4, 8], P(('section', 'dp'), 'replica'), may hold values from 1 to 48, as said below
- degrees: int32 [32, 1024], P(('section', 'dp'), 'replica'), may hold values from 1 to 4
- w_self: bfloat16 [512, 256], replicated, may hold values from -0.25 to 0.25
- w_neigh: bfloat16 [512, 256], replicated, may hold values from -0.25 to 0.25
- cotangent: bfloat16 [32, 1024, 256], P(('section', 'dp'), 'replica'), may hold values from -6 to 6
Outputs:
- hidden: bfloat16 [32, 1024, 256], P(('section', 'dp'), 'replica')
- grad_features: bfloat16 [32, 1024, 512], P(('section', 'dp'), 'replica')
- grad_self: float32 [512, 256], replicated
- grad_neigh: float32 [512, 256], replicated
The draws below stay inside these ranges and needn't reach their ends.
Inputs may be any that keep to these rules, and one draw needn't show every extreme that they name: `tile_cols`: the 48 column tile numbers of one row tile are distinct. `row_counts`: slots of a row tile from its count on are unused; every device has a row tile with all 48 slots used.
All inputs are finite; a program needn't handle non-finite values.
Results may differ from the reference program's by a relative error of at most 0.022.
Values may be sent and summed in bfloat16 or wider, within the bound.
A program may use at most 128 MiB of HBM per device.

```python
import jax
import jax.numpy as jnp
from jax import lax

F_IN = 512
F_OUT = 256
TILE = 128
ROWS_DEV = 256
PANELS = 32
NODES = 32768
RT = 8
NCT = 64
MPR = 48
N_REPLICA = 4


def draw_tile_cols(key, part):
    key = jax.random.fold_in(key, 23)
    scores = jax.random.randint(key, (PANELS, N_REPLICA, RT, NCT), 0, 1 << 20)
    scores = scores * NCT + jnp.arange(NCT, dtype=jnp.int32)
    order = jnp.argsort(scores, axis=-1)
    return order[..., :MPR].astype(jnp.int32)


def draw_row_counts(key, part):
    key = jax.random.fold_in(key, 11)
    cap_key, count_key, full_key = jax.random.split(key, 3)
    device_caps = jax.random.randint(cap_key, (PANELS, N_REPLICA, 1), MPR // 4 + 1, MPR + 1)
    counts = jax.random.randint(count_key, (PANELS, N_REPLICA, RT), 1, MPR + 1)
    counts = jnp.minimum(counts, device_caps)
    full_row = jax.random.randint(full_key, (PANELS, N_REPLICA, 1), 0, RT)
    counts = jnp.where(jnp.arange(RT, dtype=jnp.int32)[None, None, :] == full_row, MPR, counts)
    return counts.astype(jnp.int32)


def with_ends(array, rng, low, high):
    longest = array.shape.index(max(array.shape))
    spots = []
    for shift in (0, 1):
        where = [jax.random.randint(jax.random.fold_in(rng, axis), (), 0, length) for axis, length in enumerate(array.shape)]
        where[longest] = (where[longest] + shift) % array.shape[longest]
        spots.append(tuple(where))
    return array.at[spots[0]].set(low).at[spots[1]].set(high)


def block_scale(stream_key, shape, shards, low, high):
    gain, own = 1.0, jax.random.fold_in(stream_key, 6)
    for dim, parts in shards:
        heights = jnp.exp(jax.random.uniform(jax.random.fold_in(own, dim), (parts,), jnp.float32, low / len(shards), high / len(shards)))
        gain = gain * jnp.repeat(heights, shape[dim] // parts).reshape([-1 if axis == dim else 1 for axis in range(len(shape))])
    return gain


def normal_values(stream_key, extent, width, bound, cuts=(), kind=jnp.bfloat16):
    drawn = width * jax.random.normal(stream_key, extent, jnp.float32)
    if cuts:
        drawn = drawn * block_scale(stream_key, extent, cuts, -0.22, 0.18)
    return jnp.clip(drawn, -bound, bound).astype(kind)


def setup_inputs(seed: int = 0) -> dict:
    streams_of = jax.random.split(jax.random.key(seed), 9)
    features = normal_values(streams_of[0], (PANELS, N_REPLICA * ROWS_DEV, F_IN), 1.0, 6.0, ((0, 32), (1, 4)))
    tile_vals = normal_values(streams_of[1], (PANELS, N_REPLICA, RT, MPR, TILE, TILE), (MPR * TILE) ** -0.5, 0.078125, ((0, 32), (1, 4)))
    tile_cols = draw_tile_cols(jax.random.fold_in(streams_of[8], 71), 0)
    row_counts = draw_row_counts(jax.random.fold_in(streams_of[8], 71), 0)
    degrees = with_ends(jax.random.randint(streams_of[4], (PANELS, N_REPLICA * ROWS_DEV), 1, 5), jax.random.fold_in(streams_of[4], 1), 1, 4).astype(jnp.int32)
    w_self = normal_values(streams_of[5], (F_IN, F_OUT), F_IN ** -0.5, 0.25)
    w_neigh = normal_values(streams_of[6], (F_IN, F_OUT), F_IN ** -0.5, 0.25)
    cotangent = normal_values(streams_of[7], (PANELS, N_REPLICA * ROWS_DEV, F_OUT), 1.0, 6.0, ((0, 32), (1, 4)))
    return {"features": features, "tile_vals": tile_vals, "tile_cols": tile_cols, "row_counts": row_counts, "degrees": degrees, "w_self": w_self, "w_neigh": w_neigh, "cotangent": cotangent}


def silu_slope(pre_value):
    sigmoid_v = jax.nn.sigmoid(pre_value)
    return sigmoid_v * (1.0 + pre_value * (1.0 - sigmoid_v))


def reference(features, tile_vals, tile_cols, row_counts, degrees, w_self, w_neigh, cotangent):
    feature_width = features.shape[2]
    out_width = w_self.shape[1]
    col_per_dev = ROWS_DEV // TILE
    slot_live = jnp.arange(MPR, dtype=jnp.int32)[None, None, None, :] < row_counts[..., None]
    masked = tile_vals * slot_live[..., None, None].astype(tile_vals.dtype)
    col_tiles = features.reshape(PANELS, N_REPLICA, col_per_dev, TILE, feature_width)
    col_tiles = jnp.transpose(col_tiles, (1, 0, 2, 3, 4)).reshape(N_REPLICA, NCT, TILE, feature_width)
    degree_f = degrees.astype(jnp.float32)[..., None]

    def forward_one(flat_index):
        block_id = flat_index // N_REPLICA
        replica_id = flat_index % N_REPLICA
        tile_block = masked[block_id, replica_id].astype(jnp.float32)
        chosen = jnp.take(col_tiles[replica_id], tile_cols[block_id, replica_id], axis=0).astype(jnp.float32)
        partial_value = jnp.einsum("imab,imbf->iaf", tile_block, chosen)
        return partial_value.reshape(RT * TILE, feature_width).astype(jnp.bfloat16)

    partials = lax.map(forward_one, jnp.arange(PANELS * N_REPLICA, dtype=jnp.int32))
    partials = lax.optimization_barrier(partials)
    partials = partials.reshape(PANELS, N_REPLICA, RT * TILE, feature_width).astype(jnp.float32)
    aggregate = (jnp.sum(partials, axis=1) / degree_f).astype(jnp.bfloat16)

    flat_feat = features.reshape(-1, feature_width)
    flat_agg = aggregate.reshape(-1, feature_width)
    preact = jnp.dot(flat_feat, w_self, preferred_element_type=jnp.float32) + jnp.dot(flat_agg, w_neigh, preferred_element_type=jnp.float32)
    hidden = jax.nn.silu(preact).astype(jnp.bfloat16)
    grad_pre = (cotangent.reshape(-1, out_width).astype(jnp.float32) * silu_slope(preact)).astype(jnp.bfloat16)
    node_scale = NODES ** -0.5
    grad_self = jnp.dot(flat_feat.T, grad_pre, preferred_element_type=jnp.float32) * node_scale
    grad_neigh = jnp.dot(flat_agg.T, grad_pre, preferred_element_type=jnp.float32) * node_scale
    grad_agg = jnp.dot(grad_pre, w_neigh.T, preferred_element_type=jnp.float32).reshape(PANELS, N_REPLICA * ROWS_DEV, feature_width)
    grad_agg = (grad_agg / degree_f).astype(jnp.bfloat16)

    def backward_one(flat_index, carry):
        block_id = flat_index // N_REPLICA
        replica_id = flat_index % N_REPLICA
        tile_block = masked[block_id, replica_id].astype(jnp.float32)
        row_grad = grad_agg[block_id].reshape(RT, TILE, feature_width).astype(jnp.float32)
        pieces = jnp.einsum("imab,iaf->imbf", tile_block, row_grad)
        col_sums = jax.ops.segment_sum(pieces.reshape(RT * MPR, TILE, feature_width), tile_cols[block_id, replica_id].reshape(-1), num_segments=NCT)
        rounded = lax.optimization_barrier(col_sums.astype(jnp.bfloat16))
        rounded = rounded.astype(jnp.float32).reshape(PANELS, ROWS_DEV, feature_width)
        return carry.at[:, replica_id].add(rounded)

    start = jnp.zeros((PANELS, N_REPLICA, ROWS_DEV, feature_width), jnp.float32)
    back = lax.fori_loop(0, PANELS * N_REPLICA, backward_one, start)
    grad_features = jnp.dot(grad_pre, w_self.T, preferred_element_type=jnp.float32) + back.reshape(-1, feature_width)
    grad_features = grad_features.astype(jnp.bfloat16).reshape(PANELS, N_REPLICA * ROWS_DEV, feature_width)
    return hidden.reshape(PANELS, N_REPLICA * ROWS_DEV, out_width), grad_features, grad_self, grad_neigh
```

```python
import functools
import math

import jax
import jax.numpy as jnp
from jax import lax
from jax.experimental import pallas as pl
from jax.experimental.pallas import tpu as pltpu
from jax.sharding import PartitionSpec as P

MESH = pl.DeviceIdType.MESH
BF16 = jnp.bfloat16
F32 = jnp.float32
NX = 4
TILE = 128
ROWS = 256
HALF = 128
QUARTER = 64
STRIP = NX * ROWS
N_SEND = 192


def dot(a, b):
    return jnp.dot(a, b, preferred_element_type=F32)


def dot_nt(a, b):
    return lax.dot_general(a, b, (((1,), (1,)), ((), ())), preferred_element_type=F32)


class Links:
    def __init__(self, send_sem, recv_sem):
        self.send_sem, self.recv_sem, self.count, self.sent = send_sem, recv_sem, 0, []

    def send(self, src, dst, device):
        copy = pltpu.make_async_remote_copy(
            src_ref=src,
            dst_ref=dst,
            send_sem=self.send_sem.at[self.count],
            recv_sem=self.recv_sem.at[self.count],
            device_id=device,
            device_id_type=MESH,
        )
        self.count += 1
        copy.start()
        self.sent.append(copy)
        return copy

    def drain(self):
        for copy in self.sent:
            copy.wait_send()


def kernel(
    node_scale,
    x_ref, tiles_hbm, slot_ref, deg_ref, ws_ref, wn_ref, cot_ref,
    hid_ref, gf_ref, gs_ref, gn_ref,
    *scratch,
):
    row_tiles = slot_ref.shape[0]
    tile_refs, scratch = scratch[:row_tiles], scratch[row_tiles:]
    (
        bands, y_all, acc, self_pre, x_t, part_out, part_in, ht, pair_out, pair_in, sums,
        az_s, az_b, bx_s, bx_b, mid_a, mid_b, ax_s, ax_b, bz_s, bz_b, own_gf,
        *rest,
    ) = scratch
    self_bufs, neigh_bufs, (tile_sem, send_sem, recv_sem) = rest[:8], rest[8:16], rest[16:]

    section = lax.axis_index("section")
    x, core = section // 2, section % 2
    y, z = lax.axis_index("replica"), lax.axis_index("dp")
    links = Links(send_sem, recv_sem)

    def at(dx=0, dy=0, dz=0, flip=False):
        c = 1 - core if flip else core
        return {"section": lax.rem(x + dx, NX) * 2 + c, "replica": lax.rem(y + dy, NX), "dp": lax.rem(z + dz, NX)}

    plane = [(dx, dz) for dx in range(NX) for dz in range(NX) if (dx, dz) != (0, 0)]
    barrier = pltpu.get_barrier_semaphore()
    peers = [at(flip=True)] + [at(dy=d) for d in (1, 2, 3)] + [at(dx=dx, dz=dz) for dx, dz in plane]
    for peer in peers:
        pl.semaphore_signal(barrier, inc=1, device_id=peer, device_id_type=MESH)

    tile_copies = []
    slots = tile_refs[0].shape[0] - 1
    for i in range(row_tiles):
        copy = pltpu.make_async_copy(
            tiles_hbm.at[pl.ds(i * slots, slots)], tile_refs[i].at[pl.ds(0, slots)], tile_sem.at[i]
        )
        copy.start()
        tile_copies.append(copy)
        tile_refs[i][slots] = jnp.zeros((TILE, TILE), BF16)

    own = x_ref[...]
    me = (x * 2 + core) * NX + z
    y_all[pl.ds(pl.multiple_of(me * ROWS, ROWS), ROWS), :] = dot(own, wn_ref[...]).astype(BF16)
    pl.semaphore_wait(barrier, len(peers))

    def block(du, dv, h, quarter=None):
        dx, dz = (du, dv) if h == 0 else (dv, du)
        start = ((lax.rem(x + dx, NX) * 2 + core) * NX + lax.rem(z + dz, NX)) * ROWS + h * HALF
        size = HALF
        if quarter is not None:
            start, size = start + quarter * QUARTER, QUARTER
        return y_all.at[pl.ds(pl.multiple_of(start, QUARTER), size), :]

    def step(h, first, d):
        along_x = (h == 0) == first
        return at(dx=d) if along_x else at(dz=d)

    def push(h, first, d, du, dv, quarter=None):
        ref = block(du, dv, h, quarter)
        return links.send(ref, ref, step(h, first, d))

    def to_partner(h, du, dv):
        ref = block(du, dv, h)
        partner[h, du, dv] = links.send(ref, ref, at(flip=True))

    def make_rows(i):
        tile_copies[i].wait()

        def put(q, carry):
            for k in range(4):
                c = q * 4 + k
                bands[pl.ds(i * TILE, TILE), pl.ds(pl.multiple_of(c * TILE, TILE), TILE)] = tile_refs[i][slot_ref[i, c]]
            return carry

        lax.fori_loop(0, slot_ref.shape[1] // 4, put, 0)

    partner, p1, p1q, p2, p2q = {}, {}, {}, {}, {}
    for h in (0, 1):
        p1[h, 3] = push(h, True, 1, 0, 0)
        p1[h, 1] = push(h, True, 3, 0, 0)
    for h in (0, 1):
        p2[h, 0, 3] = push(h, False, 1, 0, 0)
        p2[h, 0, 1] = push(h, False, 3, 0, 0)
    for h in (0, 1):
        to_partner(h, 0, 0)

    self_pre[...] = dot(own, ws_ref[...])
    x_t[...] = own.T
    for i in range(0, 4):
        make_rows(i)

    for h in (0, 1):
        for du in (3, 1):
            p1[h, du].wait_recv()
            back = 1 if du == 3 else 3
            p1q[h, du] = push(h, True, back, du, 0, 0 if du == 3 else 1)
    for du in (3, 1):
        for h in (0, 1):
            p2[h, du, 3] = push(h, False, 1, du, 0)
            p2[h, du, 1] = push(h, False, 3, du, 0)
            to_partner(h, du, 0)
    for i in range(4, 6):
        make_rows(i)

    def relay(du):
        for h in (0, 1):
            for dv in (3, 1):
                p2[h, du, dv].wait_recv()
                p2q[h, du, dv] = push(h, False, 1 if dv == 3 else 3, du, dv, 0 if dv == 3 else 1)
                to_partner(h, du, dv)

    def finish(du):
        for h in (0, 1):
            p2q[h, du, 3].wait_recv()
            p2q[h, du, 1].wait_recv()
            to_partner(h, du, 2)

    relay(0)
    for h in (0, 1):
        p1q[h, 3].wait_recv()
        p1q[h, 1].wait_recv()
        p2[h, 2, 3] = push(h, False, 1, 2, 0)
        p2[h, 2, 1] = push(h, False, 3, 2, 0)
        to_partner(h, 2, 0)
    for i in range(6, 8):
        make_rows(i)

    def strip_of(dx, flip):
        c = 1 - core if flip else core
        return pl.ds(pl.multiple_of((lax.rem(x + dx, NX) * 2 + c) * STRIP, STRIP), STRIP)

    def spread(dx, flip, first=False):
        cols = strip_of(dx, flip)
        value = dot(bands[:, cols], y_all[cols, :])
        acc[...] = value if first else acc[...] + value

    def wait_partner(dx):
        for dz in range(NX):
            partner[0, dx, dz].wait_recv()
            partner[1, dz, dx].wait_recv()

    finish(0)
    relay(3)
    relay(1)
    finish(3)
    finish(1)
    wait_partner(0)
    spread(0, False, True)
    relay(2)
    spread(0, True)
    wait_partner(3)
    spread(3, False)
    spread(3, True)
    finish(2)
    wait_partner(1)
    spread(1, False)
    spread(1, True)
    wait_partner(2)
    own_cols, flip_cols = strip_of(2, False), strip_of(2, True)

    def last_rows(dy):
        rows = pl.ds(pl.multiple_of(lax.rem(y + dy, NX) * ROWS, ROWS), ROWS)
        return acc[rows, :] + dot(bands[rows, own_cols], y_all[own_cols, :]) + dot(bands[rows, flip_cols], y_all[flip_cols, :])

    parts = []
    for d in (2, 1, 3):
        part_out[d - 1] = last_rows(d).astype(BF16)
        parts.append(links.send(part_out.at[d - 1], part_in.at[d - 1], at(dy=d)))
    total = last_rows(0)
    deg = jnp.broadcast_to(deg_ref[...].astype(F32), (ROWS, ROWS)).T
    for part in parts:
        part.wait_recv()
    total = total + part_in[0].astype(F32) + part_in[1].astype(F32) + part_in[2].astype(F32)

    preact = self_pre[...] + total / deg
    sig = jax.nn.sigmoid(preact)
    grad_pre = (cot_ref[...].astype(F32) * (sig * (1.0 + preact * (1.0 - sig)))).astype(BF16)
    scaled = grad_pre.astype(F32) / deg
    own_rows = pl.ds(pl.multiple_of(y * ROWS, ROWS), ROWS)
    ht[:, own_rows] = scaled.T.astype(BF16)
    grads = [links.send(ht.at[:, own_rows], ht.at[:, own_rows], at(dy=d)) for d in (2, 1, 3)]
    hid_ref[...] = (preact * sig).astype(BF16)
    own_gf[...] = dot_nt(grad_pre, ws_ref[...])
    gself = dot(x_t[...], grad_pre)

    def all_sum(value, out_ref, bufs):
        a_out, a_in, b_out, b_in, c_out, c_in, c_all, result = bufs
        depth = a_in.shape[0]
        seg = depth // NX
        mine = pl.ds(pl.multiple_of(core * depth, depth), depth)
        other = pl.ds(pl.multiple_of((1 - core) * depth, depth), depth)
        a_out[...] = value.astype(BF16)
        copy = links.send(a_out.at[other, :], a_in, at(flip=True))
        yield
        copy.wait_recv()
        b_out[...] = (a_out[mine, :].astype(F32) + a_in[...].astype(F32)).astype(BF16)

        def seg_at(d, base=0):
            return pl.ds(pl.multiple_of(base + lax.rem(y + d, NX) * seg, seg), seg)

        copies = [links.send(b_out.at[seg_at(d), :], b_in.at[d - 1], at(dy=d)) for d in (2, 1, 3)]
        yield
        for copy in copies:
            copy.wait_recv()
        c_out[...] = b_out[seg_at(0), :].astype(F32) + b_in[0].astype(F32) + b_in[1].astype(F32) + b_in[2].astype(F32)

        def piece(dx, dz):
            j = lax.rem(x + dx, NX) * NX + lax.rem(z + dz, NX)
            return pl.ds(pl.multiple_of((j // 2) * 8, 8), 8), pl.ds(pl.multiple_of((j % 2) * 128, 128), 128)

        copies = [
            links.send(c_out.at[piece(dx, dz)], c_in.at[n], at(dx=dx, dz=dz)) for n, (dx, dz) in enumerate(plane)
        ]
        yield
        mine_piece = c_out[piece(0, 0)]
        for n, copy in enumerate(copies):
            copy.wait_recv()
            mine_piece = mine_piece + c_in[n]
        c_all[piece(0, 0)] = mine_piece
        copies = [links.send(c_all.at[piece(0, 0)], c_all.at[piece(0, 0)], at(dx=dx, dz=dz)) for dx, dz in plane]
        yield
        for copy in copies:
            copy.wait_recv()
        rows = seg_at(0, core * depth)
        result[rows, :] = c_all[...].astype(BF16)
        copies = [links.send(result.at[rows, :], result.at[rows, :], at(dy=d)) for d in (2, 1, 3)]
        yield
        for copy in copies:
            copy.wait_recv()
        copy = links.send(result.at[mine, :], result.at[mine, :], at(flip=True))
        yield
        copy.wait_recv()
        out_ref[...] = result[...].astype(F32) * node_scale
        yield

    self_sum = all_sum(gself, gs_ref, self_bufs)
    next(self_sum)
    for copy in grads:
        copy.wait_recv()

    def collect(dx, flip):
        return dot(ht[...], bands[:, strip_of(dx, flip)])

    def add(a, b):
        return (a.astype(F32) + b.astype(F32)).astype(BF16)

    pair, a1, a2 = {}, {}, {}
    lo, hi, half_a, half_b = pl.ds(0, QUARTER), pl.ds(QUARTER, QUARTER), pl.ds(0, HALF), pl.ds(HALF, HALF)
    b_lo, b_hi = pl.ds(HALF, QUARTER), pl.ds(HALF + QUARTER, QUARTER)

    def z_at(d):
        return lax.rem(z + d, NX)

    def give(dx):
        value = collect(dx, True).astype(BF16)
        for k in range(NX):
            pair_out[dx, k] = value[:, k * ROWS : (k + 1) * ROWS]
        pair[dx] = links.send(pair_out.at[dx], pair_in.at[dx], at(flip=True))

    def keep(dx):
        value = collect(dx, False)
        pair[dx].wait_recv()
        for k in range(NX):
            sums[dx, k] = (value[:, k * ROWS : (k + 1) * ROWS] + pair_in[dx, k].astype(F32)).astype(BF16)
        a1[dx] = (
            links.send(sums.at[dx, z_at(2), lo], az_s.at[0, dx], at(dz=1)),
            links.send(sums.at[dx, z_at(2), hi], az_s.at[1, dx], at(dz=3)),
        )

    def a_relay(dx):
        up, down = a1[dx]
        up.wait_recv()
        sums[dx, z_at(1), lo] = add(sums[dx, z_at(1), lo], az_s[0, dx])
        first = links.send(sums.at[dx, z_at(1), half_a], az_b.at[0, dx], at(dz=1))
        down.wait_recv()
        sums[dx, z_at(3), hi] = add(sums[dx, z_at(3), hi], az_s[1, dx])
        second = links.send(sums.at[dx, z_at(3), half_a], az_b.at[1, dx], at(dz=3))
        a2[dx] = (first, second)

    def a_close(dx):
        for copy in a2[dx]:
            copy.wait_recv()
        total = sums[dx, z, half_a].astype(F32) + az_b[0, dx].astype(F32) + az_b[1, dx].astype(F32)
        mid_a[dx] = total.astype(BF16)

    give(2)
    give(1)
    keep(2)
    b_up = links.send(sums.at[2, :, b_lo], bx_s.at[0], at(dx=1))
    b_down = links.send(sums.at[2, :, b_hi], bx_s.at[1], at(dx=3))
    give(3)
    next(self_sum)
    keep(1)
    b_up.wait_recv()
    for k in range(NX):
        sums[1, k, b_lo] = add(sums[1, k, b_lo], bx_s[0, k])
    b_up = links.send(sums.at[1, :, half_b], bx_b.at[0], at(dx=1))
    give(0)
    a_relay(2)
    keep(3)
    b_down.wait_recv()
    for k in range(NX):
        sums[3, k, b_hi] = add(sums[3, k, b_hi], bx_s[1, k])
    b_down = links.send(sums.at[3, :, half_b], bx_b.at[1], at(dx=3))
    a_relay(1)
    keep(0)
    a_relay(3)
    a_relay(0)
    next(self_sum)

    a_close(2)
    qa_up = links.send(mid_a.at[2, lo], ax_s.at[0], at(dx=1))
    qa_down = links.send(mid_a.at[2, hi], ax_s.at[1], at(dx=3))
    next(self_sum)
    b_up.wait_recv()
    b_down.wait_recv()
    for k in range(NX):
        total = sums[0, k, half_b].astype(F32) + bx_b[0, k].astype(F32) + bx_b[1, k].astype(F32)
        mid_b[k] = total.astype(BF16)
    qb_up = links.send(mid_b.at[z_at(2), lo], bz_s.at[0], at(dz=1))
    qb_down = links.send(mid_b.at[z_at(2), hi], bz_s.at[1], at(dz=3))
    a_close(1)
    qa_up.wait_recv()
    mid_a[1, lo] = add(mid_a[1, lo], ax_s[0])
    qa_up = links.send(mid_a.at[1], ax_b.at[0], at(dx=1))
    a_close(3)
    qa_down.wait_recv()
    mid_a[3, hi] = add(mid_a[3, hi], ax_s[1])
    qa_down = links.send(mid_a.at[3], ax_b.at[1], at(dx=3))
    next(self_sum)
    qb_up.wait_recv()
    mid_b[z_at(1), lo] = add(mid_b[z_at(1), lo], bz_s[0])
    qb_up = links.send(mid_b.at[z_at(1)], bz_b.at[0], at(dz=1))
    qb_down.wait_recv()
    mid_b[z_at(3), hi] = add(mid_b[z_at(3), hi], bz_s[1])
    qb_down = links.send(mid_b.at[z_at(3)], bz_b.at[1], at(dz=3))
    a_close(0)
    next(self_sum)
    for copy in (qa_up, qa_down, qb_up, qb_down):
        copy.wait_recv()
    sum_a = mid_a[0].astype(F32) + ax_b[0].astype(F32) + ax_b[1].astype(F32)
    sum_b = mid_b[z].astype(F32) + bz_b[0].astype(F32) + bz_b[1].astype(F32)
    back = jnp.concatenate([sum_a, sum_b], axis=0).T.astype(BF16)

    neigh_sum = all_sum(dot(x_t[...], back), gn_ref, neigh_bufs)
    next(neigh_sum)
    gf_ref[...] = (own_gf[...] + dot_nt(back, wn_ref[...])).astype(BF16)
    for _ in self_sum:
        pass
    for _ in neigh_sum:
        pass
    links.drain()


def local(features, tile_vals, tile_cols, row_counts, degrees, w_self, w_neigh, cotangent):
    f_in, f_out = w_self.shape
    _, _, row_tiles, slots = tile_cols.shape
    col_tiles = lax.axis_size(("section", "dp")) * ROWS // TILE
    nodes = lax.axis_size(("section", "replica", "dp")) * ROWS
    slot = jnp.arange(slots, dtype=jnp.int32)
    live = slot[None, :] < row_counts[0, 0][:, None]
    hit = live[:, None, :] & (tile_cols[0, 0][:, None, :] == jnp.arange(col_tiles, dtype=jnp.int32)[None, :, None])
    slot_of = jnp.min(jnp.where(hit, slot[None, None, :], slots), axis=-1)

    def vmem(*shape, dtype=BF16):
        return pltpu.VMEM(shape, dtype)

    def sum_buffers():
        depth = f_in // 2
        return [
            vmem(f_in, f_out), vmem(depth, f_out), vmem(depth, f_out), vmem(NX - 1, depth // NX, f_out),
            vmem(depth // NX, f_out, dtype=F32), vmem(NX * NX - 1, 8, 128, dtype=F32),
            vmem(depth // NX, f_out, dtype=F32), vmem(f_in, f_out),
        ]

    scratch = [vmem(slots + 1, TILE, TILE) for _ in range(row_tiles)] + [
        vmem(row_tiles * TILE, col_tiles * TILE),
        vmem(col_tiles * TILE, f_out),
        vmem(row_tiles * TILE, f_out, dtype=F32),
        vmem(ROWS, f_out, dtype=F32),
        vmem(f_in, ROWS),
        vmem(NX - 1, ROWS, f_out),
        vmem(NX - 1, ROWS, f_out),
        vmem(f_out, NX * ROWS),
        vmem(NX, NX, f_out, ROWS),
        vmem(NX, NX, f_out, ROWS),
        vmem(NX, NX, f_out, ROWS),
        vmem(2, NX, QUARTER, ROWS),
        vmem(2, NX, HALF, ROWS),
        vmem(2, NX, QUARTER, ROWS),
        vmem(2, NX, HALF, ROWS),
        vmem(NX, HALF, ROWS),
        vmem(NX, HALF, ROWS),
        vmem(2, QUARTER, ROWS),
        vmem(2, HALF, ROWS),
        vmem(2, QUARTER, ROWS),
        vmem(2, HALF, ROWS),
        vmem(ROWS, f_in, dtype=F32),
        *sum_buffers(),
        *sum_buffers(),
        pltpu.SemaphoreType.DMA((row_tiles,)),
        pltpu.SemaphoreType.DMA((N_SEND,)),
        pltpu.SemaphoreType.DMA((N_SEND,)),
    ]
    in_vmem = pl.BlockSpec(memory_space=pltpu.VMEM)
    hidden, grad_features, grad_self, grad_neigh = pl.pallas_call(
        functools.partial(kernel, 1.0 / math.sqrt(nodes)),
        out_shape=(
            jax.ShapeDtypeStruct((ROWS, f_out), BF16),
            jax.ShapeDtypeStruct((ROWS, f_in), BF16),
            jax.ShapeDtypeStruct((f_in, f_out), F32),
            jax.ShapeDtypeStruct((f_in, f_out), F32),
        ),
        in_specs=[
            in_vmem,
            pl.BlockSpec(memory_space=pl.ANY),
            pl.BlockSpec(memory_space=pltpu.SMEM),
            in_vmem, in_vmem, in_vmem, in_vmem,
        ],
        out_specs=(in_vmem,) * 4,
        scratch_shapes=scratch,
        compiler_params=pltpu.CompilerParams(
            collective_id=0, has_side_effects=True, vmem_limit_bytes=58 * 1024 * 1024
        ),
        name="sage_layer",
    )(
        features[0],
        tile_vals.reshape(row_tiles * slots, TILE, TILE),
        slot_of,
        degrees,
        w_self,
        w_neigh,
        cotangent[0],
    )
    return hidden[None], grad_features[None], grad_self, grad_neigh


def solution(mesh):
    node = P(("section", "dp"), "replica", None)
    placed = (
        node,
        P(("section", "dp"), "replica", None, None, None, None),
        P(("section", "dp"), "replica", None, None),
        P(("section", "dp"), "replica", None),
        P(("section", "dp"), "replica"),
        P(),
        P(),
        node,
    )
    return jax.shard_map(local, mesh=mesh, in_specs=placed, out_specs=(node, node, P(), P()), check_vma=False)
```

```python
import functools
import math

import jax
import jax.numpy as jnp
from jax import lax
from jax.experimental import pallas as pl
from jax.experimental.pallas import tpu as pltpu
from jax.sharding import PartitionSpec as P

MESH = pl.DeviceIdType.MESH
BF16 = jnp.bfloat16
F32 = jnp.float32
NX = 4
TILE = 128
ROWS = 256
HALF = 128
QUARTER = 64
STRIP = NX * ROWS
N_SEND = 224


def dot(a, b):
    return jnp.dot(a, b, preferred_element_type=F32)


def dot_nt(a, b):
    return lax.dot_general(a, b, (((1,), (1,)), ((), ())), preferred_element_type=F32)


class Links:
    def __init__(self, send_sem, recv_sem):
        self.send_sem, self.recv_sem, self.count, self.sent = send_sem, recv_sem, 0, []

    def send(self, src, dst, device):
        copy = pltpu.make_async_remote_copy(
            src_ref=src,
            dst_ref=dst,
            send_sem=self.send_sem.at[self.count],
            recv_sem=self.recv_sem.at[self.count],
            device_id=device,
            device_id_type=MESH,
        )
        self.count += 1
        copy.start()
        self.sent.append(copy)
        return copy

    def drain(self):
        for copy in self.sent:
            copy.wait_send()


def kernel(
    x_ref, tiles_hbm, cols_ref, counts_ref, deg_ref, ws_ref, wn_ref, cot_ref,
    hid_ref, gf_ref, gs_ref, gn_ref,
    *scratch,
):
    row_tiles, slots = cols_ref.shape
    tile_refs, scratch = scratch[:row_tiles], scratch[row_tiles:]
    (
        table, slot_ref, bands, y_all, acc, self_pre, rdeg, part_out, part_in, ht, pair_out, pair_in, sums,
        az_s, az_b, bx_s, bx_b, mid_a, mid_b, ax, bz, x_row, x_col, own_gf,
        *rest,
    ) = scratch
    self_bufs, neigh_bufs, (tile_sem, table_sem, send_sem, recv_sem) = rest[:6], rest[6:12], rest[12:]

    section = lax.axis_index("section")
    x, core = section // 2, section % 2
    y, z = lax.axis_index("replica"), lax.axis_index("dp")
    links = Links(send_sem, recv_sem)

    def place(px, pc, py, pz):
        return {"section": px * 2 + pc, "replica": py, "dp": pz}

    def at(dx=0, dy=0, dz=0, flip=False):
        return place(lax.rem(x + dx, NX), 1 - core if flip else core, lax.rem(y + dy, NX), lax.rem(z + dz, NX))

    barrier = pltpu.get_barrier_semaphore()
    peers = [at(flip=True)] + [at(dx=d) for d in (1, 3, 2)] + [at(dz=d) for d in (1, 3, 2)] + [at(dy=d) for d in (1, 3, 2)]
    for peer in peers:
        pl.semaphore_signal(barrier, inc=1, device_id=peer, device_id_type=MESH)

    tile_copies = []
    for i in range(row_tiles):
        copy = pltpu.make_async_copy(
            tiles_hbm.at[pl.ds(i * slots, slots)], tile_refs[i].at[pl.ds(0, slots)], tile_sem.at[i]
        )
        copy.start()
        tile_copies.append(copy)

    own = x_ref[...]
    me = (x * 2 + core) * NX + z
    y_all[pl.ds(pl.multiple_of(me * ROWS, ROWS), ROWS), :] = dot(own, wn_ref[...]).astype(BF16)
    pl.semaphore_wait(barrier, len(peers))

    def block(du, dv, h=None, quarter=None):
        dx, dz = (dv, du) if h == 1 else (du, dv)
        start = ((lax.rem(x + dx, NX) * 2 + core) * NX + lax.rem(z + dz, NX)) * ROWS
        size = ROWS
        if h is not None:
            start, size = start + h * HALF, HALF
        if quarter is not None:
            start, size = start + quarter * QUARTER, QUARTER
        return y_all.at[pl.ds(pl.multiple_of(start, QUARTER), size), :]

    def along(h, d):
        return at(dx=d) if h == 0 else at(dz=d)

    def push(h, d, du, dv, quarter=None):
        ref = block(du, dv, h, quarter)
        return links.send(ref, ref, along(1 - h, d))

    def to_partner(dx, dz):
        ref = block(dx, dz)
        partner[dx, dz] = links.send(ref, ref, at(flip=True))

    def make_rows(i):
        tile_copies[i].wait()

        def put(q, carry):
            for k in range(8):
                c = q * 8 + k
                bands[pl.ds(i * TILE, TILE), pl.ds(pl.multiple_of(c * TILE, TILE), TILE)] = tile_refs[i][slot_ref[i, c]]
            return carry

        lax.fori_loop(0, bands.shape[1] // TILE // 8, put, 0)

    partner, line, far, relay = {}, {}, {}, {}
    for d in (1, 3, 2):
        for h in (0, 1):
            line[h, NX - d] = links.send(block(0, 0), block(0, 0), along(h, d))
    to_partner(0, 0)

    shape = cols_ref.shape
    row_id = lax.broadcasted_iota(jnp.int32, shape, 0)
    count = jnp.zeros(shape, jnp.int32)
    for i in range(row_tiles):
        count = jnp.where(row_id == i, counts_ref[i], count)
    live = jnp.where(lax.broadcasted_iota(jnp.int32, shape, 1) < count, cols_ref[...], -1)
    col_id = lax.broadcasted_iota(jnp.int32, table.shape, 1)
    found = jnp.full(table.shape, slots, jnp.int32)
    for m in range(slots):
        found = jnp.where(live[:, m : m + 1] == col_id, m, found)
    table[...] = found
    table_copy = pltpu.make_async_copy(table, slot_ref, table_sem)
    table_copy.start()
    for i in range(row_tiles):
        tile_refs[i][slots] = jnp.zeros((TILE, TILE), BF16)
    table_copy.wait()
    for i in range(0, 4):
        make_rows(i)

    for du in (3, 1):
        for h in (0, 1):
            line[h, du].wait_recv()
            far[h, du, 3] = push(h, 1, du, 0)
            far[h, du, 1] = push(h, 3, du, 0)
            to_partner(*((du, 0) if h == 0 else (0, du)))
    self_pre[...] = dot(own, ws_ref[...])
    for i in range(4, 6):
        make_rows(i)
    for h in (0, 1):
        line[h, 2].wait_recv()
        far[h, 2, 3] = push(h, 1, 2, 0)
        far[h, 2, 1] = push(h, 3, 2, 0)
        far[h, 2, 2] = push(h, 2, 2, 0)
        to_partner(*((2, 0) if h == 0 else (0, 2)))
    for i in range(6, 8):
        make_rows(i)

    def strip_of(dx, flip):
        c = 1 - core if flip else core
        return pl.ds(pl.multiple_of((lax.rem(x + dx, NX) * 2 + c) * STRIP, STRIP), STRIP)

    def spread(dx, flip, first=False):
        if flip:
            for dz in range(NX):
                partner[dx, dz].wait_recv()
        cols = strip_of(dx, flip)
        value = dot(bands[:, cols], y_all[cols, :])
        acc[...] = value if first else acc[...] + value

    for du in (3, 1):
        for dv in (3, 1):
            for h in (0, 1):
                far[h, du, dv].wait_recv()
                relay[h, du, dv] = push(h, 1 if dv == 3 else 3, du, dv, 0 if dv == 3 else 1)
    for dx in (3, 1):
        for dz in (3, 1):
            to_partner(dx, dz)
    spread(0, False, True)
    for h in (0, 1):
        for dv in (3, 1, 2):
            far[h, 2, dv].wait_recv()
    to_partner(2, 2)
    for du in (3, 1):
        for h in (0, 1):
            relay[h, du, 3].wait_recv()
            relay[h, du, 1].wait_recv()
        to_partner(du, 2)
        to_partner(2, du)
    x_row[0] = own
    x_col[0] = own
    x_lines = []
    for d in (2, 1, 3):
        x_lines.append(links.send(x_ref, x_row.at[NX - d], at(dx=d)))
        x_lines.append(links.send(x_ref, x_col.at[NX - d], at(dz=d)))
    spread(0, True)
    spread(3, False)
    spread(1, False)
    spread(3, True)
    spread(1, True)
    rdeg[...] = 1.0 / jnp.broadcast_to(deg_ref[...].astype(F32), (ROWS, ROWS)).T
    for dz in range(NX):
        partner[2, dz].wait_recv()
    own_cols, flip_cols = strip_of(2, False), strip_of(2, True)

    def last_rows(dy):
        rows = pl.ds(pl.multiple_of(lax.rem(y + dy, NX) * ROWS, ROWS), ROWS)
        return acc[rows, :] + dot(bands[rows, own_cols], y_all[own_cols, :]) + dot(bands[rows, flip_cols], y_all[flip_cols, :])

    parts = []
    for d in (2, 1, 3):
        part_out[d - 1] = last_rows(d).astype(BF16)
        parts.append(links.send(part_out.at[d - 1], part_in.at[d - 1], at(dy=d)))
    total = last_rows(0)
    for part in parts:
        part.wait_recv()
    total = total + part_in[0].astype(F32) + part_in[1].astype(F32) + part_in[2].astype(F32)

    preact = self_pre[...] + total * rdeg[...]
    sig = jax.nn.sigmoid(preact)
    grad_pre = (cot_ref[...].astype(F32) * (sig * (1.0 + preact * (1.0 - sig)))).astype(BF16)
    own_rows = pl.ds(pl.multiple_of(y * ROWS, ROWS), ROWS)
    ht[:, own_rows] = (grad_pre.astype(F32) * rdeg[...]).T.astype(BF16)
    grads = [links.send(ht.at[:, own_rows], ht.at[:, own_rows], at(dy=d)) for d in (2, 1, 3)]
    hid_ref[...] = (preact * sig).astype(BF16)
    own_gf[...] = dot_nt(grad_pre, ws_ref[...])

    z_one, z_two = z + 1 - 2 * (z % 2), NX - 1 - z
    half_bit = lax.rem((z + 1) // 2, 2)

    def all_sum(value, out_ref, bufs):
        a_out, a_in, b_out, b_in, c_in, result = bufs
        depth = a_in.shape[0]
        seg = depth // 8
        mine = pl.ds(pl.multiple_of(core * depth, depth), depth)
        other = pl.ds(pl.multiple_of((1 - core) * depth, depth), depth)
        a_out[...] = value.astype(BF16)
        copy = links.send(a_out.at[other, :], a_in, at(flip=True))
        yield
        copy.wait_recv()
        b_out[...] = (a_out[mine, :].astype(F32) + a_in[...].astype(F32)).astype(BF16)

        def seg_at(d, flip_z, base=0):
            bit = 1 - half_bit if flip_z else half_bit
            return pl.ds(pl.multiple_of(base + (lax.rem(y + d, NX) * 2 + bit) * seg, seg), seg)

        group = [(2, True), (2, False), (1, True), (3, True), (1, False), (3, False), (0, True)]

        def first_peer(d, flip_z):
            return place(x, core, lax.rem(y + d, NX), z_one if flip_z else z)

        copies = [
            links.send(b_out.at[seg_at(*to), :], b_in.at[n], first_peer(*to)) for n, to in enumerate(group)
        ]
        yield
        piece = b_out[seg_at(0, False), :].astype(F32)
        for n, copy in enumerate(copies):
            copy.wait_recv()
            piece = piece + b_in[n].astype(F32)
        slot = x * 2 + z // 2
        c_in[slot] = piece.astype(BF16)
        copies = [
            links.send(c_in.at[slot], c_in.at[slot], place(lax.rem(x + d, NX), core, y, z_two if flip_z else z))
            for d, flip_z in group
        ]
        yield
        for copy in copies:
            copy.wait_recv()
        piece = c_in[0].astype(F32)
        for n in range(1, 8):
            piece = piece + c_in[n].astype(F32)
        rows = seg_at(0, False, core * depth)
        result[rows, :] = piece.astype(BF16)
        copies = [links.send(result.at[rows, :], result.at[rows, :], first_peer(*to)) for to in group]
        yield
        for copy in copies:
            copy.wait_recv()
        copy = links.send(result.at[mine, :], result.at[mine, :], at(flip=True))
        yield
        copy.wait_recv()
        out_ref[...] = result[...]
        yield

    self_sum = all_sum(dot(grad_pre.astype(F32).T.astype(BF16), own), gs_ref, self_bufs)
    next(self_sum)
    for copy in grads:
        copy.wait_recv()

    def collect(dx, flip):
        return dot(ht[...], bands[:, strip_of(dx, flip)])

    def add(a, b):
        return (a.astype(F32) + b.astype(F32)).astype(BF16)

    def add3(a, b, c):
        return a.astype(F32) + b.astype(F32) + c.astype(F32)

    pair, a1, a2, b1, b2, fold = {}, {}, {}, {}, {}, []
    lo, hi, half_a, half_b = pl.ds(0, QUARTER), pl.ds(QUARTER, QUARTER), pl.ds(0, HALF), pl.ds(HALF, HALF)
    b_lo, b_hi = pl.ds(HALF, QUARTER), pl.ds(HALF + QUARTER, QUARTER)

    def z_at(d):
        return lax.rem(z + d, NX)

    def give(dx):
        value = collect(dx, True).astype(BF16)
        for k in range(NX):
            pair_out[dx, k] = value[:, k * ROWS : (k + 1) * ROWS]
        pair[dx] = links.send(pair_out.at[dx], pair_in.at[dx], at(flip=True))

    def keep(dx):
        value = collect(dx, False)
        pair[dx].wait_recv()
        for k in range(NX):
            sums[dx, k] = (value[:, k * ROWS : (k + 1) * ROWS] + pair_in[dx, k].astype(F32)).astype(BF16)
        a1[dx] = (
            links.send(sums.at[dx, z_at(2), lo], az_s.at[0, dx], at(dz=1)),
            links.send(sums.at[dx, z_at(2), hi], az_s.at[1, dx], at(dz=3)),
        )

    def a_relay(dx):
        up, down = a1[dx]
        up.wait_recv()
        sums[dx, z_at(1), lo] = add(sums[dx, z_at(1), lo], az_s[0, dx])
        first = links.send(sums.at[dx, z_at(1), half_a], az_b.at[0, dx], at(dz=1))
        down.wait_recv()
        sums[dx, z_at(3), hi] = add(sums[dx, z_at(3), hi], az_s[1, dx])
        second = links.send(sums.at[dx, z_at(3), half_a], az_b.at[1, dx], at(dz=3))
        a2[dx] = (first, second)

    def a_close(dx):
        for copy in a2[dx]:
            copy.wait_recv()
        mid_a[dx] = add3(sums[dx, z, half_a], az_b[0, dx], az_b[1, dx]).astype(BF16)
        if dx:
            fold.append(links.send(mid_a.at[dx], ax.at[dx - 1], at(dx=dx)))

    def b_open():
        for dz in (2, 1, 3, 0):
            b1[dz] = (
                links.send(sums.at[2, z_at(dz), b_lo], bx_s.at[0, dz], at(dx=1)),
                links.send(sums.at[2, z_at(dz), b_hi], bx_s.at[1, dz], at(dx=3)),
            )

    def b_relay(side):
        dx, part = (1, b_lo) if side == 0 else (3, b_hi)
        for dz in (2, 1, 3, 0):
            b1[dz][side].wait_recv()
            sums[dx, z_at(dz), part] = add(sums[dx, z_at(dz), part], bx_s[side, dz])
            b2[side, dz] = links.send(sums.at[dx, z_at(dz), half_b], bx_b.at[side, dz], at(dx=dx))

    def b_close(dz):
        b2[0, dz].wait_recv()
        b2[1, dz].wait_recv()
        mid_b[dz] = add3(sums[0, z_at(dz), half_b], bx_b[0, dz], bx_b[1, dz]).astype(BF16)
        if dz:
            fold.append(links.send(mid_b.at[dz], bz.at[dz - 1], at(dz=dz)))

    give(2)
    give(1)
    keep(2)
    b_open()
    next(self_sum)
    give(3)
    keep(1)
    a_relay(2)
    b_relay(0)
    give(0)
    keep(3)
    a_relay(1)
    b_relay(1)
    keep(0)
    next(self_sum)
    a_relay(3)
    a_relay(0)
    for d in (2, 1):
        a_close(d)
        b_close(d)
    next(self_sum)
    for d in (3, 0):
        a_close(d)
        b_close(d)

    for copy in x_lines:
        copy.wait_recv()
    top, bottom = dot(mid_a[0], x_row[0]), dot(mid_b[0], x_col[0])
    for d in range(1, NX):
        top, bottom = top + dot(mid_a[d], x_row[d]), bottom + dot(mid_b[d], x_col[d])
    neigh_sum = all_sum(jnp.concatenate([top, bottom], axis=0), gn_ref, neigh_bufs)
    next(neigh_sum)
    next(self_sum)
    next(neigh_sum)
    for copy in fold:
        copy.wait_recv()
    sum_a = mid_a[0].astype(F32) + add3(ax[0], ax[1], ax[2])
    sum_b = mid_b[0].astype(F32) + add3(bz[0], bz[1], bz[2])
    back = jnp.concatenate([sum_a, sum_b], axis=0).T.astype(BF16)
    gf_ref[...] = (own_gf[...] + dot_nt(back, wn_ref[...])).astype(BF16)
    for _ in self_sum:
        pass
    for _ in neigh_sum:
        pass
    links.drain()


def finish(node_scale, hid_in, gf_in, gs_in, gn_in, hid_ref, gf_ref, gs_ref, gn_ref):
    hid_ref[...] = hid_in[...]
    gf_ref[...] = gf_in[...]
    gs_ref[...] = gs_in[...].astype(F32).T * node_scale
    gn_ref[...] = gn_in[...].astype(F32).T * node_scale


def local(features, tile_vals, tile_cols, row_counts, degrees, w_self, w_neigh, cotangent):
    f_in, f_out = w_self.shape
    _, _, row_tiles, slots = tile_cols.shape
    col_tiles = lax.axis_size(("section", "dp")) * ROWS // TILE
    nodes = lax.axis_size(("section", "replica", "dp")) * ROWS

    def vmem(*shape, dtype=BF16):
        return pltpu.VMEM(shape, dtype)

    def sum_buffers():
        depth = f_out // 2
        return [
            vmem(f_out, f_in), vmem(depth, f_in), vmem(depth, f_in), vmem(7, depth // 8, f_in),
            vmem(8, depth // 8, f_in), vmem(f_out, f_in),
        ]

    scratch = [vmem(slots + 1, TILE, TILE) for _ in range(row_tiles)] + [
        vmem(row_tiles, 128, dtype=jnp.int32),
        pltpu.SMEM((row_tiles, 128), jnp.int32),
        vmem(row_tiles * TILE, col_tiles * TILE),
        vmem(col_tiles * TILE, f_out),
        vmem(row_tiles * TILE, f_out, dtype=F32),
        vmem(ROWS, f_out, dtype=F32),
        vmem(ROWS, ROWS, dtype=F32),
        vmem(NX - 1, ROWS, f_out),
        vmem(NX - 1, ROWS, f_out),
        vmem(f_out, NX * ROWS),
        vmem(NX, NX, f_out, ROWS),
        vmem(NX, NX, f_out, ROWS),
        vmem(NX, NX, f_out, ROWS),
        vmem(2, NX, QUARTER, ROWS),
        vmem(2, NX, HALF, ROWS),
        vmem(2, NX, QUARTER, ROWS),
        vmem(2, NX, HALF, ROWS),
        vmem(NX, HALF, ROWS),
        vmem(NX, HALF, ROWS),
        vmem(NX - 1, HALF, ROWS),
        vmem(NX - 1, HALF, ROWS),
        vmem(NX, ROWS, f_in),
        vmem(NX, ROWS, f_in),
        vmem(ROWS, f_in, dtype=F32),
        *sum_buffers(),
        *sum_buffers(),
        pltpu.SemaphoreType.DMA((row_tiles,)),
        pltpu.SemaphoreType.DMA,
        pltpu.SemaphoreType.DMA((N_SEND,)),
        pltpu.SemaphoreType.DMA((N_SEND,)),
    ]
    in_vmem = pl.BlockSpec(memory_space=pltpu.VMEM)
    in_smem = pl.BlockSpec(memory_space=pltpu.SMEM)
    raw = pl.pallas_call(
        kernel,
        out_shape=(
            jax.ShapeDtypeStruct((ROWS, f_out), BF16),
            jax.ShapeDtypeStruct((ROWS, f_in), BF16),
            jax.ShapeDtypeStruct((f_out, f_in), BF16),
            jax.ShapeDtypeStruct((f_out, f_in), BF16),
        ),
        in_specs=[in_vmem, pl.BlockSpec(memory_space=pl.ANY), in_vmem, in_smem, in_vmem, in_vmem, in_vmem, in_vmem],
        out_specs=(in_vmem,) * 4,
        scratch_shapes=scratch,
        compiler_params=pltpu.CompilerParams(
            collective_id=0, has_side_effects=True, vmem_limit_bytes=58 * 1024 * 1024
        ),
        name="sage_layer",
    )(
        features[0],
        tile_vals.reshape(row_tiles * slots, TILE, TILE),
        tile_cols[0, 0],
        row_counts[0, 0],
        degrees,
        w_self,
        w_neigh,
        cotangent[0],
    )
    hidden, grad_features, grad_self, grad_neigh = pl.pallas_call(
        functools.partial(finish, 1.0 / math.sqrt(nodes)),
        out_shape=(
            jax.ShapeDtypeStruct((ROWS, f_out), BF16),
            jax.ShapeDtypeStruct((ROWS, f_in), BF16),
            jax.ShapeDtypeStruct((f_in, f_out), F32),
            jax.ShapeDtypeStruct((f_in, f_out), F32),
        ),
        in_specs=[in_vmem] * 4,
        out_specs=(in_vmem,) * 4,
        name="finish",
    )(*raw)
    return hidden[None], grad_features[None], grad_self, grad_neigh


def solution(mesh):
    node = P(("section", "dp"), "replica", None)
    placed = (
        node,
        P(("section", "dp"), "replica", None, None, None, None),
        P(("section", "dp"), "replica", None, None),
        P(("section", "dp"), "replica", None),
        P(("section", "dp"), "replica"),
        P(),
        P(),
        node,
    )
    return jax.shard_map(local, mesh=mesh, in_specs=placed, out_specs=(node, node, P(), P()), check_vma=False)
```

```python
import functools
import math

import jax
import jax.numpy as jnp
from jax import lax
from jax.experimental import pallas as pl
from jax.experimental.pallas import tpu as pltpu
from jax.sharding import PartitionSpec as P

MESH = pl.DeviceIdType.MESH
BF16 = jnp.bfloat16
F32 = jnp.float32
NX = 4
TILE = 128
ROWS = 256
HALF = 128
QUARTER = 64
STRIP = NX * ROWS
N_SEND = 24
N_RECV = 64


def dot(a, b):
    return jnp.dot(a, b, preferred_element_type=F32)


def dot_nt(a, b):
    return lax.dot_general(a, b, (((1,), (1,)), ((), ())), preferred_element_type=F32)


class Links:
    def __init__(self, send_sem, recv_sem):
        self.send_sem, self.recv_sem = send_sem, recv_sem
        self.groups, self.sent = 0, []

    def group(self):
        self.groups += 1
        return self.recv_sem.at[self.groups - 1]

    def send(self, src, dst, device, group=None):
        count = len(self.sent)
        if count >= N_SEND:
            self.sent[count - N_SEND].wait_send()
        copy = pltpu.make_async_remote_copy(
            src_ref=src,
            dst_ref=dst,
            send_sem=self.send_sem.at[count % N_SEND],
            recv_sem=self.group() if group is None else group,
            device_id=device,
            device_id_type=MESH,
        )
        copy.start()
        self.sent.append(copy)
        return copy

    def drain(self):
        for copy in self.sent[-N_SEND:]:
            copy.wait_send()


def wait_all(group, view):
    pltpu.make_async_copy(view, view, group).wait()


def kernel(
    x_hbm, tiles_hbm, cols_hbm, counts_ref, deg_hbm, ws_hbm, wn_hbm, cot_hbm,
    hid_hbm, gf_hbm, gs_hbm, gn_hbm,
    *scratch,
):
    row_tiles, slots = cols_hbm.shape
    tile_refs, scratch = scratch[:row_tiles], scratch[row_tiles:]
    (
        table, slot_ref, bands, y_all, acc, self_pre, rdeg, part_out, part_in, ht, pair_out, pair_in, sums,
        az, bx, mid_a, mid_b, ax, bz, x_row, x_col, own_gf,
        x_ref, cols_ref, deg_ref, ws_ref, wn_ref, cot_ref, hid_ref, gf_ref, gs_ref, gn_ref,
        *rest,
    ) = scratch
    self_bufs, neigh_bufs, (tile_sem, io_sem, send_sem, recv_sem) = rest[:6], rest[6:12], rest[12:]

    io_copies = []

    def io_copy(src, dst):
        copy = pltpu.make_async_copy(src, dst, io_sem.at[len(io_copies)])
        io_copies.append(copy)
        copy.start()
        return copy

    x_in, wn_in = io_copy(x_hbm, x_ref), io_copy(wn_hbm, wn_ref)

    section = lax.axis_index("section")
    x, core = section // 2, section % 2
    y, z = lax.axis_index("replica"), lax.axis_index("dp")
    links = Links(send_sem, recv_sem)

    def place(px, pc, py, pz):
        return {"section": px * 2 + pc, "replica": py, "dp": pz}

    def at(dx=0, dy=0, dz=0, flip=False):
        return place(lax.rem(x + dx, NX), 1 - core if flip else core, lax.rem(y + dy, NX), lax.rem(z + dz, NX))

    barrier = pltpu.get_barrier_semaphore()
    peers = [at(flip=True)] + [at(dx=d) for d in (1, 3, 2)] + [at(dz=d) for d in (1, 3, 2)] + [at(dy=d) for d in (1, 3, 2)]
    for peer in peers:
        pl.semaphore_signal(barrier, inc=1, device_id=peer, device_id_type=MESH)

    tile_copies = []
    for i in range(row_tiles):
        copy = pltpu.make_async_copy(
            tiles_hbm.at[pl.ds(i * slots, slots)], tile_refs[i].at[pl.ds(0, slots)], tile_sem.at[i]
        )
        copy.start()
        tile_copies.append(copy)

    cols_in, ws_in, deg_in, cot_in = (
        io_copy(cols_hbm, cols_ref), io_copy(ws_hbm, ws_ref), io_copy(deg_hbm, deg_ref), io_copy(cot_hbm, cot_ref)
    )
    x_in.wait()
    wn_in.wait()
    own = x_ref[...]
    me = (x * 2 + core) * NX + z
    y_all[pl.ds(pl.multiple_of(me * ROWS, ROWS), ROWS), :] = dot(own, wn_ref[...]).astype(BF16)
    pl.semaphore_wait(barrier, len(peers))

    def block(du, dv, h=None, quarter=None):
        dx, dz = (dv, du) if h == 1 else (du, dv)
        start = ((lax.rem(x + dx, NX) * 2 + core) * NX + lax.rem(z + dz, NX)) * ROWS
        size = ROWS
        if h is not None:
            start, size = start + h * HALF, HALF
        if quarter is not None:
            start, size = start + quarter * QUARTER, QUARTER
        return y_all.at[pl.ds(pl.multiple_of(start, QUARTER), size), :]

    def along(h, d):
        return at(dx=d) if h == 0 else at(dz=d)

    def push(h, d, du, dv, quarter=None, group=None):
        ref = block(du, dv, h, quarter)
        return links.send(ref, ref, along(1 - h, d), group)

    partner = [links.group() for _ in range(NX)]

    def to_partner(dx, dz):
        ref = block(dx, dz)
        links.send(ref, ref, at(flip=True), partner[dx])

    def make_rows(i):
        tile_copies[i].wait()

        def put(q, carry):
            for k in range(8):
                c = q * 8 + k
                bands[pl.ds(i * TILE, TILE), pl.ds(pl.multiple_of(c * TILE, TILE), TILE)] = tile_refs[i][slot_ref[i, c]]
            return carry

        lax.fori_loop(0, bands.shape[1] // TILE // 8, put, 0)

    line, far = {}, {}
    rest, far_two, relay = ([links.group() for _ in range(n)] for n in (2, 2, 4))
    def send_line(h, d, part, group=None):
        ref = block(0, 0, part)
        line[h, NX - d, part] = links.send(ref, ref, along(h, d), group)

    for d in (1, 3, 2):
        for h in (0, 1):
            send_line(h, d, h)
    to_partner(0, 0)
    for d in (1, 3):
        for h in (0, 1):
            send_line(h, d, 1 - h, rest[h])

    cols_in.wait()
    shape = cols_ref.shape
    row_id = lax.broadcasted_iota(jnp.int32, shape, 0)
    count = jnp.zeros(shape, jnp.int32)
    for i in range(row_tiles):
        count = jnp.where(row_id == i, counts_ref[i], count)
    live = jnp.where(lax.broadcasted_iota(jnp.int32, shape, 1) < count, cols_ref[...], -1)
    col_id = lax.broadcasted_iota(jnp.int32, table.shape, 1)
    found = jnp.full(table.shape, slots, jnp.int32)
    for m in range(slots):
        found = jnp.where(live[:, m : m + 1] == col_id, m, found)
    table[...] = found
    table_copy = io_copy(table, slot_ref)
    for i in range(row_tiles):
        tile_refs[i][slots] = jnp.zeros((TILE, TILE), BF16)
    table_copy.wait()
    for i in range(0, 2):
        make_rows(i)

    for du in (3, 1):
        for h in (0, 1):
            line[h, du, h].wait_recv()
            far[h, du, 3] = push(h, 1, du, 0)
            far[h, du, 1] = push(h, 3, du, 0)
    for h in (0, 1):
        send_line(h, 2, 1 - h)
    ws_in.wait()
    self_pre[...] = dot(own, ws_ref[...])
    for i in range(2, 4):
        make_rows(i)
    for h in (0, 1):
        line[h, 2, h].wait_recv()
        for d in (1, 3, 2):
            push(h, d, 2, 0, group=far_two[h])
    for h in (0, 1):
        wait_all(rest[h], y_all.at[pl.ds(0, 2 * HALF), :])
        for du in (3, 1):
            to_partner(*((du, 0) if h == 0 else (0, du)))
    for i in range(4, 6):
        make_rows(i)

    def strip_of(dx, flip):
        c = 1 - core if flip else core
        return pl.ds(pl.multiple_of((lax.rem(x + dx, NX) * 2 + c) * STRIP, STRIP), STRIP)

    def spread(dx, flip, first=False):
        cols = strip_of(dx, flip)
        if flip:
            wait_all(partner[dx], y_all.at[cols, :])
        value = dot(bands[:, cols], y_all[cols, :])
        acc[...] = value if first else acc[...] + value

    for du in (3, 1):
        for dv in (3, 1):
            for h in (0, 1):
                far[h, du, dv].wait_recv()
                push(h, 1 if dv == 3 else 3, du, dv, 0 if dv == 3 else 1, relay[h + du - 1])
    for dx in (3, 1):
        for dz in (3, 1):
            to_partner(dx, dz)
    for h in (0, 1):
        line[h, 2, 1 - h].wait_recv()
        to_partner(*((2, 0) if h == 0 else (0, 2)))
    for i in range(6, 8):
        make_rows(i)
    spread(0, False, True)
    for h in (0, 1):
        wait_all(far_two[h], y_all.at[pl.ds(0, 3 * HALF), :])
    to_partner(2, 2)
    for du in (3, 1):
        for h in (0, 1):
            wait_all(relay[h + du - 1], block(du, 2, h))
        to_partner(du, 2)
        to_partner(2, du)
    spread(0, True)
    spread(3, False)
    spread(1, False)
    spread(3, True)
    spread(1, True)
    deg_in.wait()
    cot_in.wait()
    rdeg[...] = 1.0 / jnp.broadcast_to(deg_ref[...].astype(F32), (ROWS, ROWS)).T
    own_cols, flip_cols = strip_of(2, False), strip_of(2, True)
    wait_all(partner[2], y_all.at[flip_cols, :])

    def last_rows(dy):
        rows = pl.ds(pl.multiple_of(lax.rem(y + dy, NX) * ROWS, ROWS), ROWS)
        return acc[rows, :] + dot(bands[rows, own_cols], y_all[own_cols, :]) + dot(bands[rows, flip_cols], y_all[flip_cols, :])

    parts = links.group()
    for d in (2, 1, 3):
        part_out[d - 1] = last_rows(d).astype(BF16)
        links.send(part_out.at[d - 1], part_in.at[d - 1], at(dy=d), parts)
    x_row[0] = own
    x_col[0] = own
    row_in, col_in = links.group(), links.group()
    for d in (2, 1, 3):
        links.send(x_ref, x_row.at[NX - d], at(dx=d), row_in)
        links.send(x_ref, x_col.at[NX - d], at(dz=d), col_in)
    total = last_rows(0)
    wait_all(parts, part_in)
    total = total + part_in[0].astype(F32) + part_in[1].astype(F32) + part_in[2].astype(F32)

    preact = self_pre[...] + total * rdeg[...]
    sig = jax.nn.sigmoid(preact)
    grad_pre = (cot_ref[...].astype(F32) * (sig * (1.0 + preact * (1.0 - sig)))).astype(BF16)
    own_rows = pl.ds(pl.multiple_of(y * ROWS, ROWS), ROWS)
    ht[:, own_rows] = (grad_pre.astype(F32) * rdeg[...]).T.astype(BF16)
    grads = links.group()
    for d in (2, 1, 3):
        links.send(ht.at[:, own_rows], ht.at[:, own_rows], at(dy=d), grads)
    hid_ref[...] = (preact * sig).astype(BF16)
    hid_out = io_copy(hid_ref, hid_hbm)
    own_gf[...] = dot_nt(grad_pre, ws_ref[...])

    z_one, z_two = z + 1 - 2 * (z % 2), NX - 1 - z
    half_bit = lax.rem((z + 1) // 2, 2)

    def all_sum(value, out_ref, bufs):
        a_out, a_in, b_out, b_in, c_in, result = bufs
        depth = a_in.shape[0]
        seg = depth // 8
        mine = pl.ds(pl.multiple_of(core * depth, depth), depth)
        other = pl.ds(pl.multiple_of((1 - core) * depth, depth), depth)
        a_out[...] = value.astype(BF16)
        copy = links.send(a_out.at[other, :], a_in, at(flip=True))
        yield
        copy.wait_recv()
        b_out[...] = (a_out[mine, :].astype(F32) + a_in[...].astype(F32)).astype(BF16)

        def seg_at(d, flip_z, base=0):
            bit = 1 - half_bit if flip_z else half_bit
            return pl.ds(pl.multiple_of(base + (lax.rem(y + d, NX) * 2 + bit) * seg, seg), seg)

        group = [(2, True), (2, False), (1, True), (3, True), (1, False), (3, False), (0, True)]

        def first_peer(d, flip_z):
            return place(x, core, lax.rem(y + d, NX), z_one if flip_z else z)

        arrived = links.group()
        for n, to in enumerate(group):
            links.send(b_out.at[seg_at(*to), :], b_in.at[n], first_peer(*to), arrived)
        yield
        wait_all(arrived, b_in)
        piece = b_out[seg_at(0, False), :].astype(F32)
        for n in range(7):
            piece = piece + b_in[n].astype(F32)
        slot = x * 2 + z // 2
        c_in[slot] = piece.astype(BF16)
        arrived = links.group()
        for d, flip_z in group:
            peer = place(lax.rem(x + d, NX), core, y, z_two if flip_z else z)
            links.send(c_in.at[slot], c_in.at[slot], peer, arrived)
        yield
        wait_all(arrived, c_in.at[pl.ds(0, 7)])
        piece = c_in[0].astype(F32)
        for n in range(1, 8):
            piece = piece + c_in[n].astype(F32)
        rows = seg_at(0, False, core * depth)
        result[rows, :] = piece.astype(BF16)
        arrived = links.group()
        for to in group:
            links.send(result.at[rows, :], result.at[rows, :], first_peer(*to), arrived)
        yield
        wait_all(arrived, result.at[pl.ds(0, 7 * seg), :])
        copy = links.send(result.at[mine, :], result.at[mine, :], at(flip=True))
        yield
        copy.wait_recv()
        out_ref[...] = result[...]
        yield

    self_sum = all_sum(dot(grad_pre.astype(F32).T.astype(BF16), own), gs_ref, self_bufs)
    next(self_sum)
    next(self_sum)
    wait_all(grads, ht.at[:, pl.ds(0, (NX - 1) * ROWS)])

    def collect(dx, flip):
        return dot(ht[...], bands[:, strip_of(dx, flip)])

    def add3(a, b, c):
        return a.astype(F32) + b.astype(F32) + c.astype(F32)

    pair, a_lines = {}, [links.group() for _ in range(NX)]
    b_lines, a_fold, b_fold = links.group(), links.group(), links.group()
    half_a, half_b = pl.ds(0, HALF), pl.ds(HALF, HALF)

    def z_at(d):
        return lax.rem(z + d, NX)

    def give(dx):
        value = collect(dx, True).astype(BF16)
        for k in range(NX):
            pair_out[dx, k] = value[:, k * ROWS : (k + 1) * ROWS]
        pair[dx] = links.send(pair_out.at[dx], pair_in.at[dx], at(flip=True))

    def keep(dx):
        value = collect(dx, False)
        pair[dx].wait_recv()
        for k in range(NX):
            sums[dx, k] = (value[:, k * ROWS : (k + 1) * ROWS] + pair_in[dx, k].astype(F32)).astype(BF16)
        for d in (2, 1, 3):
            links.send(sums.at[dx, z_at(d), half_a], az.at[dx, d - 1], at(dz=d), a_lines[dx])
        if dx:
            links.send(sums.at[dx, :, half_b], bx.at[dx - 1], at(dx=dx), b_lines)

    def a_close(dx):
        wait_all(a_lines[dx], az.at[dx])
        total = sums[dx, z, half_a].astype(F32) + add3(az[dx, 0], az[dx, 1], az[dx, 2])
        mid_a[dx] = total.astype(BF16)
        if dx:
            links.send(mid_a.at[dx], ax.at[dx - 1], at(dx=dx), a_fold)

    def b_close(dz):
        total = sums[0, z_at(dz), half_b].astype(F32) + add3(bx[0, z_at(dz)], bx[1, z_at(dz)], bx[2, z_at(dz)])
        mid_b[dz] = total.astype(BF16)
        if dz:
            links.send(mid_b.at[dz], bz.at[dz - 1], at(dz=dz), b_fold)

    give(2)
    give(1)
    keep(2)
    give(3)
    keep(1)
    give(0)
    keep(3)
    keep(0)
    next(self_sum)
    a_close(2)
    a_close(1)
    a_close(3)
    wait_all(b_lines, bx)
    for d in (2, 1, 3, 0):
        b_close(d)
    a_close(0)

    wait_all(row_in, x_row.at[pl.ds(1, NX - 1)])
    wait_all(col_in, x_col.at[pl.ds(1, NX - 1)])
    top, bottom = dot(mid_a[0], x_row[0]), dot(mid_b[0], x_col[0])
    for d in range(1, NX):
        top, bottom = top + dot(mid_a[d], x_row[d]), bottom + dot(mid_b[d], x_col[d])
    neigh_sum = all_sum(jnp.concatenate([top, bottom], axis=0), gn_ref, neigh_bufs)
    next(neigh_sum)
    next(self_sum)
    next(neigh_sum)
    next(self_sum)
    wait_all(a_fold, ax)
    wait_all(b_fold, bz)
    sum_a = mid_a[0].astype(F32) + add3(ax[0], ax[1], ax[2])
    sum_b = mid_b[0].astype(F32) + add3(bz[0], bz[1], bz[2])
    back = jnp.concatenate([sum_a, sum_b], axis=0).T.astype(BF16)
    gf_ref[...] = (own_gf[...] + dot_nt(back, wn_ref[...])).astype(BF16)
    gf_out = io_copy(gf_ref, gf_hbm)
    for _ in self_sum:
        pass
    gs_out = io_copy(gs_ref, gs_hbm)
    for _ in neigh_sum:
        pass
    gn_out = io_copy(gn_ref, gn_hbm)
    links.drain()
    for copy in (hid_out, gf_out, gs_out, gn_out):
        copy.wait()


def finish(node_scale, hid_in, gf_in, gs_in, gn_in, hid_ref, gf_ref, gs_ref, gn_ref):
    hid_ref[...] = hid_in[...]
    gf_ref[...] = gf_in[...]
    gs_ref[...] = gs_in[...].astype(F32).T * node_scale
    gn_ref[...] = gn_in[...].astype(F32).T * node_scale


def local(features, tile_vals, tile_cols, row_counts, degrees, w_self, w_neigh, cotangent):
    f_in, f_out = w_self.shape
    _, _, row_tiles, slots = tile_cols.shape
    col_tiles = lax.axis_size(("section", "dp")) * ROWS // TILE
    nodes = lax.axis_size(("section", "replica", "dp")) * ROWS

    def vmem(*shape, dtype=BF16):
        return pltpu.VMEM(shape, dtype)

    def sum_buffers():
        depth = f_out // 2
        return [
            vmem(f_out, f_in), vmem(depth, f_in), vmem(depth, f_in), vmem(7, depth // 8, f_in),
            vmem(8, depth // 8, f_in), vmem(f_out, f_in),
        ]

    scratch = [vmem(slots + 1, TILE, TILE) for _ in range(row_tiles)] + [
        vmem(row_tiles, 128, dtype=jnp.int32),
        pltpu.SMEM((row_tiles, 128), jnp.int32),
        vmem(row_tiles * TILE, col_tiles * TILE),
        vmem(col_tiles * TILE, f_out),
        vmem(row_tiles * TILE, f_out, dtype=F32),
        vmem(ROWS, f_out, dtype=F32),
        vmem(ROWS, ROWS, dtype=F32),
        vmem(NX - 1, ROWS, f_out),
        vmem(NX - 1, ROWS, f_out),
        vmem(f_out, NX * ROWS),
        vmem(NX, NX, f_out, ROWS),
        vmem(NX, NX, f_out, ROWS),
        vmem(NX, NX, f_out, ROWS),
        vmem(NX, NX - 1, HALF, ROWS),
        vmem(NX - 1, NX, HALF, ROWS),
        vmem(NX, HALF, ROWS),
        vmem(NX, HALF, ROWS),
        vmem(NX - 1, HALF, ROWS),
        vmem(NX - 1, HALF, ROWS),
        vmem(NX, ROWS, f_in),
        vmem(NX, ROWS, f_in),
        vmem(ROWS, f_in, dtype=F32),
        vmem(ROWS, f_in),
        vmem(row_tiles, slots, dtype=jnp.int32),
        vmem(1, ROWS, dtype=jnp.int32),
        vmem(f_in, f_out),
        vmem(f_in, f_out),
        vmem(ROWS, f_out),
        vmem(ROWS, f_out),
        vmem(ROWS, f_in),
        vmem(f_out, f_in),
        vmem(f_out, f_in),
        *sum_buffers(),
        *sum_buffers(),
        pltpu.SemaphoreType.DMA((row_tiles,)),
        pltpu.SemaphoreType.DMA((16,)),
        pltpu.SemaphoreType.DMA((N_SEND,)),
        pltpu.SemaphoreType.DMA((N_RECV,)),
    ]
    in_vmem = pl.BlockSpec(memory_space=pltpu.VMEM)
    in_smem = pl.BlockSpec(memory_space=pltpu.SMEM)
    in_any = pl.BlockSpec(memory_space=pl.ANY)
    raw = pl.pallas_call(
        kernel,
        out_shape=(
            jax.ShapeDtypeStruct((ROWS, f_out), BF16),
            jax.ShapeDtypeStruct((ROWS, f_in), BF16),
            jax.ShapeDtypeStruct((f_out, f_in), BF16),
            jax.ShapeDtypeStruct((f_out, f_in), BF16),
        ),
        in_specs=[in_any, in_any, in_any, in_smem, in_any, in_any, in_any, in_any],
        out_specs=(in_any,) * 4,
        scratch_shapes=scratch,
        compiler_params=pltpu.CompilerParams(
            collective_id=0, has_side_effects=True, vmem_limit_bytes=58 * 1024 * 1024
        ),
        name="sage_layer",
    )(
        features[0],
        tile_vals.reshape(row_tiles * slots, TILE, TILE),
        tile_cols[0, 0],
        row_counts[0, 0],
        degrees,
        w_self,
        w_neigh,
        cotangent[0],
    )
    hidden, grad_features, grad_self, grad_neigh = pl.pallas_call(
        functools.partial(finish, 1.0 / math.sqrt(nodes)),
        out_shape=(
            jax.ShapeDtypeStruct((ROWS, f_out), BF16),
            jax.ShapeDtypeStruct((ROWS, f_in), BF16),
            jax.ShapeDtypeStruct((f_in, f_out), F32),
            jax.ShapeDtypeStruct((f_in, f_out), F32),
        ),
        in_specs=[in_vmem] * 4,
        out_specs=(in_vmem,) * 4,
        name="finish",
    )(*raw)
    return hidden[None], grad_features[None], grad_self, grad_neigh


def solution(mesh):
    node = P(("section", "dp"), "replica", None)
    placed = (
        node,
        P(("section", "dp"), "replica", None, None, None, None),
        P(("section", "dp"), "replica", None, None),
        P(("section", "dp"), "replica", None),
        P(("section", "dp"), "replica"),
        P(),
        P(),
        node,
    )
    return jax.shard_map(local, mesh=mesh, in_specs=placed, out_specs=(node, node, P(), P()), check_vma=False)
```

```python
import functools
import math

import jax
import jax.numpy as jnp
from jax import lax
from jax.experimental import pallas as pl
from jax.experimental.pallas import tpu as pltpu
from jax.sharding import PartitionSpec as P

MESH = pl.DeviceIdType.MESH
BF16 = jnp.bfloat16
F32 = jnp.float32
NX = 4
TILE = 128
ROWS = 256
HALF = 128
QUARTER = 64
STRIP = NX * ROWS
N_SEND = 24
N_RECV = 66


def dot(a, b):
    return jnp.dot(a, b, preferred_element_type=F32)


def dot_nt(a, b):
    return lax.dot_general(a, b, (((1,), (1,)), ((), ())), preferred_element_type=F32)


class Links:
    def __init__(self, send_sem, recv_sem):
        self.send_sem, self.recv_sem = send_sem, recv_sem
        self.groups, self.sent = 0, []

    def group(self):
        self.groups += 1
        assert self.groups <= N_RECV
        return self.recv_sem.at[self.groups - 1]

    def send(self, src, dst, device, group=None):
        count = len(self.sent)
        if count >= N_SEND:
            self.sent[count - N_SEND].wait_send()
        copy = pltpu.make_async_remote_copy(
            src_ref=src,
            dst_ref=dst,
            send_sem=self.send_sem.at[count % N_SEND],
            recv_sem=self.group() if group is None else group,
            device_id=device,
            device_id_type=MESH,
        )
        copy.start()
        self.sent.append(copy)
        return copy

    def drain(self):
        for copy in self.sent[-N_SEND:]:
            copy.wait_send()


def wait_all(group, view):
    pltpu.make_async_copy(view, view, group).wait()


def kernel(
    x_hbm, tiles_hbm, cols_hbm, counts_ref, deg_hbm, ws_hbm, wn_hbm, cot_hbm,
    hid_hbm, gf_hbm, gs_hbm, gn_hbm,
    *scratch,
):
    row_tiles, slots = cols_hbm.shape
    tile_refs, scratch = scratch[:row_tiles], scratch[row_tiles:]
    (
        table, slot_ref, bands, y_all, acc, self_pre, rdeg, part_out, part_in, ht, pair_out, pair_in, sums,
        az, bx, mid_a, mid_b, ax, bz, x_all, own_gf,
        cols_ref, deg_ref, ws_ref, wn_ref, cot_ref, hid_ref, gf_ref, gs_ref, gn_ref,
        *rest,
    ) = scratch
    self_bufs, neigh_bufs, (tile_sem, io_sem, send_sem, recv_sem) = rest[:6], rest[6:12], rest[12:]

    io_copies = []

    def io_copy(src, dst):
        copy = pltpu.make_async_copy(src, dst, io_sem.at[len(io_copies)])
        io_copies.append(copy)
        copy.start()
        return copy


    section = lax.axis_index("section")
    x, core = section // 2, section % 2
    y, z = lax.axis_index("replica"), lax.axis_index("dp")
    links = Links(send_sem, recv_sem)

    def x_block(dx, dz, h=None, quarter=None):
        start = (lax.rem(x + dx, NX) * NX + lax.rem(z + dz, NX)) * ROWS
        size = ROWS
        if h is not None:
            start, size = start + h * HALF, HALF
        if quarter is not None:
            start, size = start + quarter * QUARTER, QUARTER
        return x_all.at[pl.ds(pl.multiple_of(start, QUARTER), size), :]

    x_own = x_block(0, 0)
    x_in, wn_in = io_copy(x_hbm, x_own), io_copy(wn_hbm, wn_ref)

    def place(px, pc, py, pz):
        return {"section": px * 2 + pc, "replica": py, "dp": pz}

    def at(dx=0, dy=0, dz=0, flip=False):
        return place(lax.rem(x + dx, NX), 1 - core if flip else core, lax.rem(y + dy, NX), lax.rem(z + dz, NX))

    barrier = pltpu.get_barrier_semaphore()
    peers = [at(flip=True)] + [at(dx=d) for d in (1, 3, 2)] + [at(dz=d) for d in (1, 3, 2)] + [at(dy=d) for d in (1, 3, 2)]
    for peer in peers:
        pl.semaphore_signal(barrier, inc=1, device_id=peer, device_id_type=MESH)

    tile_copies = []
    for i in range(row_tiles):
        copy = pltpu.make_async_copy(
            tiles_hbm.at[pl.ds(i * slots, slots)], tile_refs[i].at[pl.ds(0, slots)], tile_sem.at[i]
        )
        copy.start()
        tile_copies.append(copy)

    cols_in, ws_in, deg_in, cot_in = (
        io_copy(cols_hbm, cols_ref), io_copy(ws_hbm, ws_ref), io_copy(deg_hbm, deg_ref), io_copy(cot_hbm, cot_ref)
    )
    x_in.wait()
    wn_in.wait()
    own = x_own[...]
    me = (x * 2 + core) * NX + z
    y_all[pl.ds(pl.multiple_of(me * ROWS, ROWS), ROWS), :] = dot(own, wn_ref[...]).astype(BF16)
    pl.semaphore_wait(barrier, len(peers))

    def block(du, dv, h=None, quarter=None):
        dx, dz = (dv, du) if h == 1 else (du, dv)
        start = ((lax.rem(x + dx, NX) * 2 + core) * NX + lax.rem(z + dz, NX)) * ROWS
        size = ROWS
        if h is not None:
            start, size = start + h * HALF, HALF
        if quarter is not None:
            start, size = start + quarter * QUARTER, QUARTER
        return y_all.at[pl.ds(pl.multiple_of(start, QUARTER), size), :]

    def along(h, d):
        return at(dx=d) if h == 0 else at(dz=d)

    def push(h, d, du, dv, quarter=None, group=None):
        ref = block(du, dv, h, quarter)
        return links.send(ref, ref, along(1 - h, d), group)

    partner = [links.group() for _ in range(NX)]

    def to_partner(dx, dz):
        ref = block(dx, dz)
        links.send(ref, ref, at(flip=True), partner[dx])

    def make_rows(i):
        tile_copies[i].wait()

        def put(q, carry):
            for k in range(8):
                c = q * 8 + k
                bands[pl.ds(i * TILE, TILE), pl.ds(pl.multiple_of(c * TILE, TILE), TILE)] = tile_refs[i][slot_ref[i, c]]
            return carry

        lax.fori_loop(0, bands.shape[1] // TILE // 8, put, 0)

    line, far = {}, {}
    rest, far_two, relay = ([links.group() for _ in range(n)] for n in (2, 2, 4))
    def send_line(h, d, part, group=None):
        ref = block(0, 0, part)
        line[h, NX - d, part] = links.send(ref, ref, along(h, d), group)

    for d in (1, 3, 2):
        for h in (0, 1):
            send_line(h, d, h)
    to_partner(0, 0)
    for d in (1, 3):
        for h in (0, 1):
            send_line(h, d, 1 - h, rest[h])

    cols_in.wait()
    shape = cols_ref.shape
    row_id = lax.broadcasted_iota(jnp.int32, shape, 0)
    count = jnp.zeros(shape, jnp.int32)
    for i in range(row_tiles):
        count = jnp.where(row_id == i, counts_ref[i], count)
    live = jnp.where(lax.broadcasted_iota(jnp.int32, shape, 1) < count, cols_ref[...], -1)
    col_id = lax.broadcasted_iota(jnp.int32, table.shape, 1)
    found = jnp.full(table.shape, slots, jnp.int32)
    for m in range(slots):
        found = jnp.where(live[:, m : m + 1] == col_id, m, found)
    table[...] = found
    table_copy = io_copy(table, slot_ref)
    for i in range(row_tiles):
        tile_refs[i][slots] = jnp.zeros((TILE, TILE), BF16)
    table_copy.wait()
    for i in range(0, 2):
        make_rows(i)

    for du in (3, 1):
        for h in (0, 1):
            line[h, du, h].wait_recv()
            far[h, du, 3] = push(h, 1, du, 0)
            far[h, du, 1] = push(h, 3, du, 0)
    for h in (0, 1):
        send_line(h, 2, 1 - h)
    ws_in.wait()
    self_pre[...] = dot(own, ws_ref[...])
    for i in range(2, 4):
        make_rows(i)
    for h in (0, 1):
        line[h, 2, h].wait_recv()
        for d in (1, 3, 2):
            push(h, d, 2, 0, group=far_two[h])
    for h in (0, 1):
        wait_all(rest[h], y_all.at[pl.ds(0, 2 * HALF), :])
        for du in (3, 1):
            to_partner(*((du, 0) if h == 0 else (0, du)))
    for i in range(4, 6):
        make_rows(i)

    def strip_of(dx, flip):
        c = 1 - core if flip else core
        return pl.ds(pl.multiple_of((lax.rem(x + dx, NX) * 2 + c) * STRIP, STRIP), STRIP)

    def spread(dx, flip, first=False):
        cols = strip_of(dx, flip)
        if flip:
            wait_all(partner[dx], y_all.at[cols, :])
        value = dot(bands[:, cols], y_all[cols, :])
        acc[...] = value if first else acc[...] + value

    for du in (3, 1):
        for dv in (3, 1):
            for h in (0, 1):
                far[h, du, dv].wait_recv()
                push(h, 1 if dv == 3 else 3, du, dv, 0 if dv == 3 else 1, relay[h + du - 1])
    for dx in (3, 1):
        for dz in (3, 1):
            to_partner(dx, dz)
    for h in (0, 1):
        line[h, 2, 1 - h].wait_recv()
        to_partner(*((2, 0) if h == 0 else (0, 2)))
    for i in range(6, 8):
        make_rows(i)
    spread(0, False, True)
    for h in (0, 1):
        wait_all(far_two[h], y_all.at[pl.ds(0, 3 * HALF), :])
    to_partner(2, 2)
    for du in (3, 1):
        for h in (0, 1):
            wait_all(relay[h + du - 1], block(du, 2, h))
        to_partner(du, 2)
        to_partner(2, du)
    x_line, x_far = {}, {}
    x_late = links.group()

    def x_push(h, d, du, dv=0, quarter=None, group=None):
        ref = x_block(*((du, dv) if h == 0 else (dv, du)), h, quarter)
        return links.send(ref, ref, along(1 - h, d), group)

    for d in (1, 3, 2):
        for h in (0, 1):
            ref = x_block(0, 0, h)
            x_line[h, NX - d] = links.send(ref, ref, along(h, d))
    for d in (1, 3, 2):
        for h in (0, 1):
            ref = x_block(0, 0, 1 - h)
            links.send(ref, ref, along(h, d), x_late)
    spread(0, True)
    spread(3, False)
    spread(1, False)
    spread(3, True)
    spread(1, True)
    deg_in.wait()
    cot_in.wait()
    rdeg[...] = 1.0 / jnp.broadcast_to(deg_ref[...].astype(F32), (ROWS, ROWS)).T
    own_cols, flip_cols = strip_of(2, False), strip_of(2, True)
    wait_all(partner[2], y_all.at[flip_cols, :])

    def last_rows(dy):
        rows = pl.ds(pl.multiple_of(lax.rem(y + dy, NX) * ROWS, ROWS), ROWS)
        return acc[rows, :] + dot(bands[rows, own_cols], y_all[own_cols, :]) + dot(bands[rows, flip_cols], y_all[flip_cols, :])

    parts = links.group()
    for d in (2, 1, 3):
        part_out[d - 1] = last_rows(d).astype(BF16)
        links.send(part_out.at[d - 1], part_in.at[d - 1], at(dy=d), parts)
    for du in (3, 1):
        for h in (0, 1):
            x_line[h, du].wait_recv()
            for d in (1, 3):
                x_far[h, du, NX - d] = x_push(h, d, du)
    for h in (0, 1):
        x_line[h, 2].wait_recv()
        for d in (1, 3, 2):
            x_push(h, d, 2, group=x_late)
    total = last_rows(0)
    wait_all(parts, part_in)
    total = total + part_in[0].astype(F32) + part_in[1].astype(F32) + part_in[2].astype(F32)

    preact = self_pre[...] + total * rdeg[...]
    sig = jax.nn.sigmoid(preact)
    grad_pre = (cot_ref[...].astype(F32) * (sig * (1.0 + preact * (1.0 - sig)))).astype(BF16)
    own_rows = pl.ds(pl.multiple_of(y * ROWS, ROWS), ROWS)
    ht[:, own_rows] = (grad_pre.astype(F32) * rdeg[...]).T.astype(BF16)
    grads = links.group()
    for d in (2, 1, 3):
        links.send(ht.at[:, own_rows], ht.at[:, own_rows], at(dy=d), grads)
    hid_ref[...] = (preact * sig).astype(BF16)
    hid_out = io_copy(hid_ref, hid_hbm)
    own_gf[...] = dot_nt(grad_pre, ws_ref[...])

    z_one, z_two = z + 1 - 2 * (z % 2), NX - 1 - z
    half_bit = lax.rem((z + 1) // 2, 2)

    def all_sum(value, out_ref, bufs):
        a_out, a_in, b_out, b_in, c_in, result = bufs
        depth = a_in.shape[0]
        seg = depth // 8
        mine = pl.ds(pl.multiple_of(core * depth, depth), depth)
        other = pl.ds(pl.multiple_of((1 - core) * depth, depth), depth)
        a_out[...] = value.astype(BF16)
        copy = links.send(a_out.at[other, :], a_in, at(flip=True))
        yield
        copy.wait_recv()
        b_out[...] = (a_out[mine, :].astype(F32) + a_in[...].astype(F32)).astype(BF16)

        def seg_at(d, flip_z, base=0):
            bit = 1 - half_bit if flip_z else half_bit
            return pl.ds(pl.multiple_of(base + (lax.rem(y + d, NX) * 2 + bit) * seg, seg), seg)

        group = [(2, True), (2, False), (1, True), (3, True), (1, False), (3, False), (0, True)]

        def first_peer(d, flip_z):
            return place(x, core, lax.rem(y + d, NX), z_one if flip_z else z)

        arrived = links.group()
        for n, to in enumerate(group):
            links.send(b_out.at[seg_at(*to), :], b_in.at[n], first_peer(*to), arrived)
        yield
        wait_all(arrived, b_in)
        piece = b_out[seg_at(0, False), :].astype(F32)
        for n in range(7):
            piece = piece + b_in[n].astype(F32)
        slot = x * 2 + z // 2
        c_in[slot] = piece.astype(BF16)
        arrived = links.group()
        for d, flip_z in group:
            peer = place(lax.rem(x + d, NX), core, y, z_two if flip_z else z)
            links.send(c_in.at[slot], c_in.at[slot], peer, arrived)
        yield
        wait_all(arrived, c_in.at[pl.ds(0, 7)])
        piece = c_in[0].astype(F32)
        for n in range(1, 8):
            piece = piece + c_in[n].astype(F32)
        rows = seg_at(0, False, core * depth)
        result[rows, :] = piece.astype(BF16)
        arrived = links.group()
        for to in group:
            links.send(result.at[rows, :], result.at[rows, :], first_peer(*to), arrived)
        yield
        wait_all(arrived, result.at[pl.ds(0, 7 * seg), :])
        copy = links.send(result.at[mine, :], result.at[mine, :], at(flip=True))
        yield
        copy.wait_recv()
        out_ref[...] = result[...]
        yield

    self_sum = all_sum(dot(grad_pre.astype(F32).T.astype(BF16), own), gs_ref, self_bufs)
    next(self_sum)
    next(self_sum)
    for du in (3, 1):
        for dv in (3, 1):
            for h in (0, 1):
                x_far[h, du, dv].wait_recv()
                x_push(h, 1 if dv == 3 else 3, du, dv, 0 if dv == 3 else 1, x_late)
    wait_all(grads, ht.at[:, pl.ds(0, (NX - 1) * ROWS)])

    def collect(dx, flip):
        return dot(ht[...], bands[:, strip_of(dx, flip)])

    def add3(a, b, c):
        return a.astype(F32) + b.astype(F32) + c.astype(F32)

    pair, a_lines = {}, [links.group() for _ in range(NX)]
    b_lines, a_fold, b_fold = links.group(), links.group(), links.group()
    half_a, half_b = pl.ds(0, HALF), pl.ds(HALF, HALF)

    def z_at(d):
        return lax.rem(z + d, NX)

    def give(dx):
        value = collect(dx, True).astype(BF16)
        for k in range(NX):
            pair_out[dx, k] = value[:, k * ROWS : (k + 1) * ROWS]
        pair[dx] = links.send(pair_out.at[dx], pair_in.at[dx], at(flip=True))

    def keep(dx):
        value = collect(dx, False)
        pair[dx].wait_recv()
        for k in range(NX):
            sums[dx, k] = (value[:, k * ROWS : (k + 1) * ROWS] + pair_in[dx, k].astype(F32)).astype(BF16)
        for d in (2, 1, 3):
            links.send(sums.at[dx, z_at(d), half_a], az.at[dx, d - 1], at(dz=d), a_lines[dx])
        if dx:
            links.send(sums.at[dx, :, half_b], bx.at[dx - 1], at(dx=dx), b_lines)

    def a_close(dx):
        wait_all(a_lines[dx], az.at[dx])
        total = sums[dx, z, half_a].astype(F32) + add3(az[dx, 0], az[dx, 1], az[dx, 2])
        mid_a[dx] = total.astype(BF16)
        if dx:
            links.send(mid_a.at[dx], ax.at[dx - 1], at(dx=dx), a_fold)

    def b_close(dz):
        total = sums[0, z_at(dz), half_b].astype(F32) + add3(bx[0, z_at(dz)], bx[1, z_at(dz)], bx[2, z_at(dz)])
        mid_b[dz] = total.astype(BF16)
        if dz:
            links.send(mid_b.at[dz], bz.at[dz - 1], at(dz=dz), b_fold)

    give(2)
    give(1)
    keep(2)
    give(3)
    keep(1)
    give(0)
    keep(3)
    keep(0)

    wait_all(x_late, x_all.at[pl.ds(0, 12 * HALF + 8 * QUARTER), :])

    def x_strip(dx):
        return x_all[pl.ds(pl.multiple_of(lax.rem(x + dx, NX) * STRIP, STRIP), STRIP), :]

    term = dot(jnp.concatenate([sums[0, k] for k in range(NX)], axis=1), x_strip(0))
    for dx in range(1, NX):
        term = term + dot(jnp.concatenate([sums[dx, k] for k in range(NX)], axis=1), x_strip(dx))
    neigh_sum = all_sum(term, gn_ref, neigh_bufs)
    next(neigh_sum)
    next(self_sum)
    next(neigh_sum)
    a_close(2)
    a_close(1)
    a_close(3)
    wait_all(b_lines, bx)
    for d in (2, 1, 3, 0):
        b_close(d)
    a_close(0)
    next(self_sum)
    next(neigh_sum)
    wait_all(a_fold, ax)
    wait_all(b_fold, bz)
    sum_a = mid_a[0].astype(F32) + add3(ax[0], ax[1], ax[2])
    sum_b = mid_b[0].astype(F32) + add3(bz[0], bz[1], bz[2])
    back = jnp.concatenate([sum_a, sum_b], axis=0).T.astype(BF16)
    gf_ref[...] = (own_gf[...] + dot_nt(back, wn_ref[...])).astype(BF16)
    gf_out = io_copy(gf_ref, gf_hbm)
    for _ in self_sum:
        pass
    gs_out = io_copy(gs_ref, gs_hbm)
    for _ in neigh_sum:
        pass
    gn_out = io_copy(gn_ref, gn_hbm)
    links.drain()
    for copy in (hid_out, gf_out, gs_out, gn_out):
        copy.wait()


def finish(node_scale, hid_in, gf_in, gs_in, gn_in, hid_ref, gf_ref, gs_ref, gn_ref):
    hid_ref[...] = hid_in[...]
    gf_ref[...] = gf_in[...]
    gs_ref[...] = gs_in[...].astype(F32).T * node_scale
    gn_ref[...] = gn_in[...].astype(F32).T * node_scale


def local(features, tile_vals, tile_cols, row_counts, degrees, w_self, w_neigh, cotangent):
    f_in, f_out = w_self.shape
    _, _, row_tiles, slots = tile_cols.shape
    col_tiles = lax.axis_size(("section", "dp")) * ROWS // TILE
    nodes = lax.axis_size(("section", "replica", "dp")) * ROWS

    def vmem(*shape, dtype=BF16):
        return pltpu.VMEM(shape, dtype)

    def sum_buffers():
        depth = f_out // 2
        return [
            vmem(f_out, f_in), vmem(depth, f_in), vmem(depth, f_in), vmem(7, depth // 8, f_in),
            vmem(8, depth // 8, f_in), vmem(f_out, f_in),
        ]

    scratch = [vmem(slots + 1, TILE, TILE) for _ in range(row_tiles)] + [
        vmem(row_tiles, 128, dtype=jnp.int32),
        pltpu.SMEM((row_tiles, 128), jnp.int32),
        vmem(row_tiles * TILE, col_tiles * TILE),
        vmem(col_tiles * TILE, f_out),
        vmem(row_tiles * TILE, f_out, dtype=F32),
        vmem(ROWS, f_out, dtype=F32),
        vmem(ROWS, ROWS, dtype=F32),
        vmem(NX - 1, ROWS, f_out),
        vmem(NX - 1, ROWS, f_out),
        vmem(f_out, NX * ROWS),
        vmem(NX, NX, f_out, ROWS),
        vmem(NX, NX, f_out, ROWS),
        vmem(NX, NX, f_out, ROWS),
        vmem(NX, NX - 1, HALF, ROWS),
        vmem(NX - 1, NX, HALF, ROWS),
        vmem(NX, HALF, ROWS),
        vmem(NX, HALF, ROWS),
        vmem(NX - 1, HALF, ROWS),
        vmem(NX - 1, HALF, ROWS),
        vmem(NX * STRIP, f_in),
        vmem(ROWS, f_in, dtype=F32),
        vmem(row_tiles, slots, dtype=jnp.int32),
        vmem(1, ROWS, dtype=jnp.int32),
        vmem(f_in, f_out),
        vmem(f_in, f_out),
        vmem(ROWS, f_out),
        vmem(ROWS, f_out),
        vmem(ROWS, f_in),
        vmem(f_out, f_in),
        vmem(f_out, f_in),
        *sum_buffers(),
        *sum_buffers(),
        pltpu.SemaphoreType.DMA((row_tiles,)),
        pltpu.SemaphoreType.DMA((16,)),
        pltpu.SemaphoreType.DMA((N_SEND,)),
        pltpu.SemaphoreType.DMA((N_RECV,)),
    ]
    in_vmem = pl.BlockSpec(memory_space=pltpu.VMEM)
    in_smem = pl.BlockSpec(memory_space=pltpu.SMEM)
    in_any = pl.BlockSpec(memory_space=pl.ANY)
    raw = pl.pallas_call(
        kernel,
        out_shape=(
            jax.ShapeDtypeStruct((ROWS, f_out), BF16),
            jax.ShapeDtypeStruct((ROWS, f_in), BF16),
            jax.ShapeDtypeStruct((f_out, f_in), BF16),
            jax.ShapeDtypeStruct((f_out, f_in), BF16),
        ),
        in_specs=[in_any, in_any, in_any, in_smem, in_any, in_any, in_any, in_any],
        out_specs=(in_any,) * 4,
        scratch_shapes=scratch,
        compiler_params=pltpu.CompilerParams(
            collective_id=0, has_side_effects=True, vmem_limit_bytes=58 * 1024 * 1024
        ),
        name="sage_layer",
    )(
        features[0],
        tile_vals.reshape(row_tiles * slots, TILE, TILE),
        tile_cols[0, 0],
        row_counts[0, 0],
        degrees,
        w_self,
        w_neigh,
        cotangent[0],
    )
    hidden, grad_features, grad_self, grad_neigh = pl.pallas_call(
        functools.partial(finish, 1.0 / math.sqrt(nodes)),
        out_shape=(
            jax.ShapeDtypeStruct((ROWS, f_out), BF16),
            jax.ShapeDtypeStruct((ROWS, f_in), BF16),
            jax.ShapeDtypeStruct((f_in, f_out), F32),
            jax.ShapeDtypeStruct((f_in, f_out), F32),
        ),
        in_specs=[in_vmem] * 4,
        out_specs=(in_vmem,) * 4,
        name="finish",
    )(*raw)
    return hidden[None], grad_features[None], grad_self, grad_neigh


def solution(mesh):
    node = P(("section", "dp"), "replica", None)
    placed = (
        node,
        P(("section", "dp"), "replica", None, None, None, None),
        P(("section", "dp"), "replica", None, None),
        P(("section", "dp"), "replica", None),
        P(("section", "dp"), "replica"),
        P(),
        P(),
        node,
    )
    return jax.shard_map(local, mesh=mesh, in_specs=placed, out_specs=(node, node, P(), P()), check_vma=False)
```

```python
import functools
import math

import jax
import jax.numpy as jnp
from jax import lax
from jax.experimental import pallas as pl
from jax.experimental.pallas import tpu as pltpu
from jax.sharding import PartitionSpec as P

MESH = pl.DeviceIdType.MESH
BF16 = jnp.bfloat16
F32 = jnp.float32
NX = 4
TILE = 128
ROWS = 256
HALF = 128
QUARTER = 64
STRIP = NX * ROWS
N_SEND = 24
N_RECV = 74


def dot(a, b):
    return jnp.dot(a, b, preferred_element_type=F32)


def dot_nt(a, b):
    return lax.dot_general(a, b, (((1,), (1,)), ((), ())), preferred_element_type=F32)


class Links:
    def __init__(self, send_sem, recv_sem):
        self.send_sem, self.recv_sem = send_sem, recv_sem
        self.groups, self.sent = 0, []

    def group(self):
        self.groups += 1
        assert self.groups <= N_RECV
        return self.recv_sem.at[self.groups - 1]

    def send(self, src, dst, device, group=None):
        count = len(self.sent)
        if count >= N_SEND:
            self.sent[count - N_SEND].wait_send()
        copy = pltpu.make_async_remote_copy(
            src_ref=src,
            dst_ref=dst,
            send_sem=self.send_sem.at[count % N_SEND],
            recv_sem=self.group() if group is None else group,
            device_id=device,
            device_id_type=MESH,
        )
        copy.start()
        self.sent.append(copy)
        return copy

    def drain(self):
        for copy in self.sent[-N_SEND:]:
            copy.wait_send()


def wait_all(group, view):
    pltpu.make_async_copy(view, view, group).wait()


def kernel(
    x_hbm, tiles_hbm, cols_hbm, counts_ref, deg_hbm, ws_hbm, wn_hbm, cot_hbm,
    hid_hbm, gf_hbm, gs_hbm, gn_hbm,
    *scratch,
):
    row_tiles, slots = cols_hbm.shape
    tile_refs, scratch = scratch[:row_tiles], scratch[row_tiles:]
    (
        table, slot_ref, bands, y_all, acc, self_pre, rdeg, part_out, part_in, pre_out, ht, pair_out, pair_in, sums,
        az, bx, mid_a, mid_b, ax, bz, x_all, own_gf,
        cols_ref, deg_ref, ws_ref, wn_ref, cot_ref, hid_ref, gf_ref, gs_ref, gn_ref,
        *rest,
    ) = scratch
    self_bufs, neigh_bufs, (tile_sem, io_sem, send_sem, recv_sem) = rest[:6], rest[6:12], rest[12:]

    io_copies = []

    def io_copy(src, dst):
        copy = pltpu.make_async_copy(src, dst, io_sem.at[len(io_copies)])
        io_copies.append(copy)
        copy.start()
        return copy


    section = lax.axis_index("section")
    x, core = section // 2, section % 2
    y, z = lax.axis_index("replica"), lax.axis_index("dp")
    links = Links(send_sem, recv_sem)

    def x_block(dx, dz, h=None, quarter=None):
        start = (lax.rem(x + dx, NX) * NX + lax.rem(z + dz, NX)) * ROWS
        size = ROWS
        if h is not None:
            start, size = start + h * HALF, HALF
        if quarter is not None:
            start, size = start + quarter * QUARTER, QUARTER
        return x_all.at[pl.ds(pl.multiple_of(start, QUARTER), size), :]

    x_own = x_block(0, 0)
    x_in, wn_in = io_copy(x_hbm, x_own), io_copy(wn_hbm, wn_ref)

    def place(px, pc, py, pz):
        return {"section": px * 2 + pc, "replica": py, "dp": pz}

    def at(dx=0, dy=0, dz=0, flip=False):
        return place(lax.rem(x + dx, NX), 1 - core if flip else core, lax.rem(y + dy, NX), lax.rem(z + dz, NX))

    barrier = pltpu.get_barrier_semaphore()
    peers = [at(flip=True)] + [at(dx=d) for d in (1, 3, 2)] + [at(dz=d) for d in (1, 3, 2)] + [at(dy=d) for d in (1, 3, 2)]
    for peer in peers:
        pl.semaphore_signal(barrier, inc=1, device_id=peer, device_id_type=MESH)

    tile_copies = []
    for i in range(row_tiles):
        copy = pltpu.make_async_copy(
            tiles_hbm.at[pl.ds(i * slots, slots)], tile_refs[i].at[pl.ds(0, slots)], tile_sem.at[i]
        )
        copy.start()
        tile_copies.append(copy)

    cols_in, ws_in, deg_in, cot_in = (
        io_copy(cols_hbm, cols_ref), io_copy(ws_hbm, ws_ref), io_copy(deg_hbm, deg_ref), io_copy(cot_hbm, cot_ref)
    )
    x_in.wait()
    wn_in.wait()
    own = x_own[...]
    me = (x * 2 + core) * NX + z
    y_all[pl.ds(pl.multiple_of(me * ROWS, ROWS), ROWS), :] = dot(own, wn_ref[...]).astype(BF16)
    pl.semaphore_wait(barrier, len(peers))

    def block(du, dv, h=None, quarter=None):
        dx, dz = (dv, du) if h == 1 else (du, dv)
        start = ((lax.rem(x + dx, NX) * 2 + core) * NX + lax.rem(z + dz, NX)) * ROWS
        size = ROWS
        if h is not None:
            start, size = start + h * HALF, HALF
        if quarter is not None:
            start, size = start + quarter * QUARTER, QUARTER
        return y_all.at[pl.ds(pl.multiple_of(start, QUARTER), size), :]

    def along(h, d):
        return at(dx=d) if h == 0 else at(dz=d)

    def push(h, d, du, dv, quarter=None, group=None):
        ref = block(du, dv, h, quarter)
        return links.send(ref, ref, along(1 - h, d), group)

    partner = [links.group() for _ in range(NX)]

    def to_partner(dx, dz):
        ref = block(dx, dz)
        links.send(ref, ref, at(flip=True), partner[dx])

    def make_rows(i):
        tile_copies[i].wait()

        def put(q, carry):
            for k in range(8):
                c = q * 8 + k
                bands[pl.ds(i * TILE, TILE), pl.ds(pl.multiple_of(c * TILE, TILE), TILE)] = tile_refs[i][slot_ref[i, c]]
            return carry

        lax.fori_loop(0, bands.shape[1] // TILE // 8, put, 0)

    line, far = {}, {}
    rest, far_two, relay = ([links.group() for _ in range(n)] for n in (2, 2, 4))
    def send_line(h, d, part, group=None):
        ref = block(0, 0, part)
        line[h, NX - d, part] = links.send(ref, ref, along(h, d), group)

    for d in (1, 3, 2):
        for h in (0, 1):
            send_line(h, d, h)
    to_partner(0, 0)
    for d in (1, 3):
        for h in (0, 1):
            send_line(h, d, 1 - h, rest[h])

    cols_in.wait()
    shape = cols_ref.shape
    row_id = lax.broadcasted_iota(jnp.int32, shape, 0)
    count = jnp.zeros(shape, jnp.int32)
    for i in range(row_tiles):
        count = jnp.where(row_id == i, counts_ref[i], count)
    live = jnp.where(lax.broadcasted_iota(jnp.int32, shape, 1) < count, cols_ref[...], -1)
    col_id = lax.broadcasted_iota(jnp.int32, table.shape, 1)
    found = jnp.full(table.shape, slots, jnp.int32)
    for m in range(slots):
        found = jnp.where(live[:, m : m + 1] == col_id, m, found)
    table[...] = found
    table_copy = io_copy(table, slot_ref)
    for i in range(row_tiles):
        tile_refs[i][slots] = jnp.zeros((TILE, TILE), BF16)
    table_copy.wait()
    for i in range(0, 2):
        make_rows(i)

    for du in (3, 1):
        for h in (0, 1):
            line[h, du, h].wait_recv()
            far[h, du, 3] = push(h, 1, du, 0)
            far[h, du, 1] = push(h, 3, du, 0)
    for h in (0, 1):
        send_line(h, 2, 1 - h)
    ws_in.wait()
    self_pre[...] = dot(own, ws_ref[...])
    for i in range(2, 4):
        make_rows(i)
    for h in (0, 1):
        line[h, 2, h].wait_recv()
        for d in (1, 3, 2):
            push(h, d, 2, 0, group=far_two[h])
    for h in (0, 1):
        wait_all(rest[h], y_all.at[pl.ds(0, 2 * HALF), :])
        for du in (3, 1):
            to_partner(*((du, 0) if h == 0 else (0, du)))
    for i in range(4, 6):
        make_rows(i)

    def strip_of(dx, flip):
        c = 1 - core if flip else core
        return pl.ds(pl.multiple_of((lax.rem(x + dx, NX) * 2 + c) * STRIP, STRIP), STRIP)

    def spread(dx, flip, first=False):
        cols = strip_of(dx, flip)
        if flip:
            wait_all(partner[dx], y_all.at[cols, :])
        value = dot(bands[:, cols], y_all[cols, :])
        acc[...] = value if first else acc[...] + value

    for du in (3, 1):
        for dv in (3, 1):
            for h in (0, 1):
                far[h, du, dv].wait_recv()
                push(h, 1 if dv == 3 else 3, du, dv, 0 if dv == 3 else 1, relay[h + du - 1])
    for dx in (3, 1):
        for dz in (3, 1):
            to_partner(dx, dz)
    for h in (0, 1):
        line[h, 2, 1 - h].wait_recv()
        to_partner(*((2, 0) if h == 0 else (0, 2)))
    for i in range(6, 8):
        make_rows(i)
    spread(0, False, True)
    for h in (0, 1):
        wait_all(far_two[h], y_all.at[pl.ds(0, 3 * HALF), :])
    to_partner(2, 2)
    for du in (3, 1):
        for h in (0, 1):
            wait_all(relay[h + du - 1], block(du, 2, h))
        to_partner(du, 2)
        to_partner(2, du)
    x_line, x_far = {}, {}
    x_late = links.group()

    def x_push(h, d, du, dv=0, quarter=None, group=None):
        ref = x_block(*((du, dv) if h == 0 else (dv, du)), h, quarter)
        return links.send(ref, ref, along(1 - h, d), group)

    x_rest, x_two = ([links.group() for _ in range(2)] for _ in range(2))

    def x_on(h, half, du, group):
        ref = x_block(*((du, 0) if h == 0 else (0, du)), half, 0 if du == 3 else 1)
        links.send(ref, ref, along(h, 1 if du == 3 else 3), group)

    def x_relay(du):
        for dv in (3, 1):
            for h in (0, 1):
                x_far[h, du, dv].wait_recv()
                x_push(h, 1 if dv == 3 else 3, du, dv, 0 if dv == 3 else 1, x_late)

    for d in (1, 3):
        for h in (0, 1):
            ref = x_block(0, 0, h)
            x_line[h, NX - d] = links.send(ref, ref, along(h, d))
    for d in (1, 3):
        for h in (0, 1):
            ref = x_block(0, 0, 1 - h)
            links.send(ref, ref, along(h, d), x_rest[h])
    spread(0, True)
    spread(3, False)
    spread(1, False)
    spread(3, True)
    spread(1, True)
    deg_in.wait()
    cot_in.wait()
    rdeg[...] = 1.0 / jnp.broadcast_to(deg_ref[...].astype(F32), (HALF, ROWS)).T
    own_cols, flip_cols = strip_of(2, False), strip_of(2, True)
    wait_all(partner[2], y_all.at[flip_cols, :])

    def add3(a, b, c):
        return a.astype(F32) + b.astype(F32) + c.astype(F32)

    def last_rows(dy):
        rows = pl.ds(pl.multiple_of(lax.rem(y + dy, NX) * ROWS, ROWS), ROWS)
        return acc[rows, :] + dot(bands[rows, own_cols], y_all[own_cols, :]) + dot(bands[rows, flip_cols], y_all[flip_cols, :])

    parts, grads = [links.group() for _ in range(2)], [links.group() for _ in range(2)]

    def send_part(f, d):
        links.send(part_out.at[f, d - 1], part_in.at[f, d - 1], at(dy=d), parts[f])

    for d in (2, 1, 3):
        value = last_rows(d).astype(BF16)
        part_out[0, d - 1] = value[:, :HALF]
        part_out[1, d - 1] = value[:, HALF:]
        send_part(0, d)
    for d in (2, 1, 3):
        send_part(1, d)
    for du in (3, 1):
        for h in (0, 1):
            x_line[h, du].wait_recv()
            x_on(h, h, du, x_two[h])
    for du in (3, 1):
        for h in (0, 1):
            for d in (1, 3):
                x_far[h, du, NX - d] = x_push(h, d, du)
    acc[pl.ds(0, ROWS), :] = last_rows(0)
    for h in (0, 1):
        wait_all(x_rest[h], x_all.at[pl.ds(0, 2 * HALF), :])
        for du in (3, 1):
            x_on(h, 1 - h, du, x_late)
    for h in (0, 1):
        wait_all(x_two[h], x_block(*((2, 0) if h == 0 else (0, 2)), h))
        for d in (1, 3):
            x_far[h, 2, NX - d] = x_push(h, d, 2)

    own_rows = pl.ds(pl.multiple_of(y * ROWS, ROWS), ROWS)
    for f in range(2):
        cols = pl.ds(f * HALF, HALF)
        wait_all(parts[f], part_in.at[f])
        total = acc[pl.ds(0, ROWS), cols] + add3(part_in[f, 0], part_in[f, 1], part_in[f, 2])
        preact = self_pre[:, cols] + total * rdeg[...]
        sig = jax.nn.sigmoid(preact)
        slope = sig * (1.0 + preact * (1.0 - sig))
        half_pre = (cot_ref[:, cols].astype(F32) * slope).astype(BF16)
        ht[cols, own_rows] = (half_pre.astype(F32) * rdeg[...]).T.astype(BF16)
        for d in (2, 1, 3):
            links.send(ht.at[cols, own_rows], ht.at[cols, own_rows], at(dy=d), grads[f])
        pre_out[:, cols] = half_pre
        hid_ref[:, cols] = (preact * sig).astype(BF16)
    hid_out = io_copy(hid_ref, hid_hbm)
    grad_pre = pre_out[...]
    own_gf[...] = dot_nt(grad_pre, ws_ref[...])

    z_one, z_two = z + 1 - 2 * (z % 2), NX - 1 - z
    half_bit = lax.rem((z + 1) // 2, 2)

    def all_sum(value, out_ref, bufs):
        a_out, a_in, b_out, b_in, c_in, result = bufs
        depth = a_in.shape[0]
        seg = depth // 8
        mine = pl.ds(pl.multiple_of(core * depth, depth), depth)
        other = pl.ds(pl.multiple_of((1 - core) * depth, depth), depth)
        a_out[...] = value.astype(BF16)
        copy = links.send(a_out.at[other, :], a_in, at(flip=True))
        yield
        copy.wait_recv()
        b_out[...] = (a_out[mine, :].astype(F32) + a_in[...].astype(F32)).astype(BF16)

        def seg_at(d, flip_z, base=0):
            bit = 1 - half_bit if flip_z else half_bit
            return pl.ds(pl.multiple_of(base + (lax.rem(y + d, NX) * 2 + bit) * seg, seg), seg)

        group = [(2, True), (2, False), (1, True), (3, True), (1, False), (3, False), (0, True)]

        def first_peer(d, flip_z):
            return place(x, core, lax.rem(y + d, NX), z_one if flip_z else z)

        arrived = links.group()
        for n, to in enumerate(group):
            links.send(b_out.at[seg_at(*to), :], b_in.at[n], first_peer(*to), arrived)
        yield
        wait_all(arrived, b_in)
        piece = b_out[seg_at(0, False), :].astype(F32)
        for n in range(7):
            piece = piece + b_in[n].astype(F32)
        slot = x * 2 + z // 2
        c_in[slot] = piece.astype(BF16)
        arrived = links.group()
        for d, flip_z in group:
            peer = place(lax.rem(x + d, NX), core, y, z_two if flip_z else z)
            links.send(c_in.at[slot], c_in.at[slot], peer, arrived)
        yield
        wait_all(arrived, c_in.at[pl.ds(0, 7)])
        piece = c_in[0].astype(F32)
        for n in range(1, 8):
            piece = piece + c_in[n].astype(F32)
        rows = seg_at(0, False, core * depth)
        result[rows, :] = piece.astype(BF16)
        arrived = links.group()
        for to in group:
            links.send(result.at[rows, :], result.at[rows, :], first_peer(*to), arrived)
        yield
        wait_all(arrived, result.at[pl.ds(0, 7 * seg), :])
        copy = links.send(result.at[mine, :], result.at[mine, :], at(flip=True))
        yield
        copy.wait_recv()
        out_ref[...] = result[...]
        yield

    self_sum = all_sum(dot(grad_pre.astype(F32).T.astype(BF16), own), gs_ref, self_bufs)
    next(self_sum)
    next(self_sum)
    x_relay(3)
    x_relay(1)
    for f in range(2):
        wait_all(grads[f], ht.at[pl.ds(f * HALF, HALF), pl.ds(0, (NX - 1) * ROWS)])

    def collect(dx, flip):
        return dot(ht[...], bands[:, strip_of(dx, flip)])

    pair, a_lines = {}, [links.group() for _ in range(NX)]
    b_lines, a_fold, b_fold = links.group(), links.group(), links.group()
    half_a, half_b = pl.ds(0, HALF), pl.ds(HALF, HALF)

    def z_at(d):
        return lax.rem(z + d, NX)

    def give(dx):
        value = collect(dx, True).astype(BF16)
        for k in range(NX):
            pair_out[dx, k] = value[:, k * ROWS : (k + 1) * ROWS]
        pair[dx] = links.send(pair_out.at[dx], pair_in.at[dx], at(flip=True))

    def keep(dx):
        value = collect(dx, False)
        pair[dx].wait_recv()
        for k in range(NX):
            sums[dx, k] = (value[:, k * ROWS : (k + 1) * ROWS] + pair_in[dx, k].astype(F32)).astype(BF16)
        for d in (2, 1, 3):
            links.send(sums.at[dx, z_at(d), half_a], az.at[dx, d - 1], at(dz=d), a_lines[dx])
        if dx:
            links.send(sums.at[dx, :, half_b], bx.at[dx - 1], at(dx=dx), b_lines)

    def a_close(dx):
        wait_all(a_lines[dx], az.at[dx])
        total = sums[dx, z, half_a].astype(F32) + add3(az[dx, 0], az[dx, 1], az[dx, 2])
        mid_a[dx] = total.astype(BF16)
        if dx:
            links.send(mid_a.at[dx], ax.at[dx - 1], at(dx=dx), a_fold)

    def b_close(dz):
        total = sums[0, z_at(dz), half_b].astype(F32) + add3(bx[0, z_at(dz)], bx[1, z_at(dz)], bx[2, z_at(dz)])
        mid_b[dz] = total.astype(BF16)
        if dz:
            links.send(mid_b.at[dz], bz.at[dz - 1], at(dz=dz), b_fold)

    give(2)
    give(1)
    x_relay(2)
    keep(2)
    give(3)
    keep(1)
    give(0)
    keep(3)
    keep(0)

    wait_all(x_late, x_all.at[pl.ds(0, 16 * QUARTER), :])

    def x_strip(dx):
        return x_all[pl.ds(pl.multiple_of(lax.rem(x + dx, NX) * STRIP, STRIP), STRIP), :]

    term = dot(jnp.concatenate([sums[0, k] for k in range(NX)], axis=1), x_strip(0))
    for dx in range(1, NX):
        term = term + dot(jnp.concatenate([sums[dx, k] for k in range(NX)], axis=1), x_strip(dx))
    neigh_sum = all_sum(term, gn_ref, neigh_bufs)
    next(neigh_sum)
    next(self_sum)
    next(neigh_sum)
    a_close(2)
    a_close(1)
    next(neigh_sum)
    a_close(3)
    wait_all(b_lines, bx)
    for d in (2, 1, 3, 0):
        b_close(d)
    a_close(0)
    next(self_sum)
    next(neigh_sum)
    wait_all(a_fold, ax)
    wait_all(b_fold, bz)
    sum_a = mid_a[0].astype(F32) + add3(ax[0], ax[1], ax[2])
    sum_b = mid_b[0].astype(F32) + add3(bz[0], bz[1], bz[2])
    back = jnp.concatenate([sum_a, sum_b], axis=0).T.astype(BF16)
    gf_ref[...] = (own_gf[...] + dot_nt(back, wn_ref[...])).astype(BF16)
    gf_out = io_copy(gf_ref, gf_hbm)
    for _ in self_sum:
        pass
    gs_out = io_copy(gs_ref, gs_hbm)
    for _ in neigh_sum:
        pass
    gn_out = io_copy(gn_ref, gn_hbm)
    links.drain()
    for copy in (hid_out, gf_out, gs_out, gn_out):
        copy.wait()


def finish(node_scale, hid_in, gf_in, gs_in, gn_in, hid_ref, gf_ref, gs_ref, gn_ref):
    hid_ref[...] = hid_in[...]
    gf_ref[...] = gf_in[...]
    gs_ref[...] = gs_in[...].astype(F32).T * node_scale
    gn_ref[...] = gn_in[...].astype(F32).T * node_scale


def local(features, tile_vals, tile_cols, row_counts, degrees, w_self, w_neigh, cotangent):
    f_in, f_out = w_self.shape
    _, _, row_tiles, slots = tile_cols.shape
    col_tiles = lax.axis_size(("section", "dp")) * ROWS // TILE
    nodes = lax.axis_size(("section", "replica", "dp")) * ROWS

    def vmem(*shape, dtype=BF16):
        return pltpu.VMEM(shape, dtype)

    def sum_buffers():
        depth = f_out // 2
        return [
            vmem(f_out, f_in), vmem(depth, f_in), vmem(depth, f_in), vmem(7, depth // 8, f_in),
            vmem(8, depth // 8, f_in), vmem(f_out, f_in),
        ]

    scratch = [vmem(slots + 1, TILE, TILE) for _ in range(row_tiles)] + [
        vmem(row_tiles, 128, dtype=jnp.int32),
        pltpu.SMEM((row_tiles, 128), jnp.int32),
        vmem(row_tiles * TILE, col_tiles * TILE),
        vmem(col_tiles * TILE, f_out),
        vmem(row_tiles * TILE, f_out, dtype=F32),
        vmem(ROWS, f_out, dtype=F32),
        vmem(ROWS, HALF, dtype=F32),
        vmem(2, NX - 1, ROWS, HALF),
        vmem(2, NX - 1, ROWS, HALF),
        vmem(ROWS, f_out),
        vmem(f_out, NX * ROWS),
        vmem(NX, NX, f_out, ROWS),
        vmem(NX, NX, f_out, ROWS),
        vmem(NX, NX, f_out, ROWS),
        vmem(NX, NX - 1, HALF, ROWS),
        vmem(NX - 1, NX, HALF, ROWS),
        vmem(NX, HALF, ROWS),
        vmem(NX, HALF, ROWS),
        vmem(NX - 1, HALF, ROWS),
        vmem(NX - 1, HALF, ROWS),
        vmem(NX * STRIP, f_in),
        vmem(ROWS, f_in, dtype=F32),
        vmem(row_tiles, slots, dtype=jnp.int32),
        vmem(1, ROWS, dtype=jnp.int32),
        vmem(f_in, f_out),
        vmem(f_in, f_out),
        vmem(ROWS, f_out),
        vmem(ROWS, f_out),
        vmem(ROWS, f_in),
        vmem(f_out, f_in),
        vmem(f_out, f_in),
        *sum_buffers(),
        *sum_buffers(),
        pltpu.SemaphoreType.DMA((row_tiles,)),
        pltpu.SemaphoreType.DMA((16,)),
        pltpu.SemaphoreType.DMA((N_SEND,)),
        pltpu.SemaphoreType.DMA((N_RECV,)),
    ]
    in_vmem = pl.BlockSpec(memory_space=pltpu.VMEM)
    in_smem = pl.BlockSpec(memory_space=pltpu.SMEM)
    in_any = pl.BlockSpec(memory_space=pl.ANY)
    raw = pl.pallas_call(
        kernel,
        out_shape=(
            jax.ShapeDtypeStruct((ROWS, f_out), BF16),
            jax.ShapeDtypeStruct((ROWS, f_in), BF16),
            jax.ShapeDtypeStruct((f_out, f_in), BF16),
            jax.ShapeDtypeStruct((f_out, f_in), BF16),
        ),
        in_specs=[in_any, in_any, in_any, in_smem, in_any, in_any, in_any, in_any],
        out_specs=(in_any,) * 4,
        scratch_shapes=scratch,
        compiler_params=pltpu.CompilerParams(
            collective_id=0, has_side_effects=True, vmem_limit_bytes=58 * 1024 * 1024
        ),
        name="sage_layer",
    )(
        features[0],
        tile_vals.reshape(row_tiles * slots, TILE, TILE),
        tile_cols[0, 0],
        row_counts[0, 0],
        degrees,
        w_self,
        w_neigh,
        cotangent[0],
    )
    hidden, grad_features, grad_self, grad_neigh = pl.pallas_call(
        functools.partial(finish, 1.0 / math.sqrt(nodes)),
        out_shape=(
            jax.ShapeDtypeStruct((ROWS, f_out), BF16),
            jax.ShapeDtypeStruct((ROWS, f_in), BF16),
            jax.ShapeDtypeStruct((f_in, f_out), F32),
            jax.ShapeDtypeStruct((f_in, f_out), F32),
        ),
        in_specs=[in_vmem] * 4,
        out_specs=(in_vmem,) * 4,
        name="finish",
    )(*raw)
    return hidden[None], grad_features[None], grad_self, grad_neigh


def solution(mesh):
    node = P(("section", "dp"), "replica", None)
    placed = (
        node,
        P(("section", "dp"), "replica", None, None, None, None),
        P(("section", "dp"), "replica", None, None),
        P(("section", "dp"), "replica", None),
        P(("section", "dp"), "replica"),
        P(),
        P(),
        node,
    )
    return jax.shard_map(local, mesh=mesh, in_specs=placed, out_specs=(node, node, P(), P()), check_vma=False)
```

```python
import functools
import math

import jax
import jax.numpy as jnp
from jax import lax
from jax.experimental import pallas as pl
from jax.experimental.pallas import tpu as pltpu
from jax.sharding import PartitionSpec as P

MESH = pl.DeviceIdType.MESH
BF16 = jnp.bfloat16
F32 = jnp.float32
NX = 4
TILE = 128
ROWS = 256
HALF = 128
QUARTER = 64
STRIP = NX * ROWS
N_SEND = 24
N_RECV = 74


def dot(a, b):
    return jnp.dot(a, b, preferred_element_type=F32)


def dot_nt(a, b):
    return lax.dot_general(a, b, (((1,), (1,)), ((), ())), preferred_element_type=F32)


class Links:
    def __init__(self, send_sem, recv_sem):
        self.send_sem, self.recv_sem = send_sem, recv_sem
        self.groups, self.sent = 0, []

    def group(self):
        self.groups += 1
        assert self.groups <= N_RECV
        return self.recv_sem.at[self.groups - 1]

    def send(self, src, dst, device, group=None):
        count = len(self.sent)
        if count >= N_SEND:
            self.sent[count - N_SEND].wait_send()
        copy = pltpu.make_async_remote_copy(
            src_ref=src,
            dst_ref=dst,
            send_sem=self.send_sem.at[count % N_SEND],
            recv_sem=self.group() if group is None else group,
            device_id=device,
            device_id_type=MESH,
        )
        copy.start()
        self.sent.append(copy)
        return copy

    def drain(self):
        for copy in self.sent[-N_SEND:]:
            copy.wait_send()


def wait_all(group, view):
    pltpu.make_async_copy(view, view, group).wait()


def kernel(
    x_hbm, tiles_hbm, cols_hbm, counts_ref, deg_hbm, ws_hbm, wn_hbm, cot_hbm,
    hid_hbm, gf_hbm, gs_hbm, gn_hbm,
    *scratch,
):
    row_tiles, slots = cols_hbm.shape
    tile_refs, scratch = scratch[:row_tiles], scratch[row_tiles:]
    (
        table, slot_ref, bands, y_all, acc, self_pre, rdeg, part_out, part_in, pre_out, ht, pair_out, pair_in, sums,
        az, bx, mid_a, mid_b, ax, bz, x_all, own_gf,
        cols_ref, deg_ref, ws_ref, wn_ref, cot_ref, hid_ref, gf_ref, gs_ref, gn_ref,
        *rest,
    ) = scratch
    self_bufs, neigh_bufs, (tile_sem, io_sem, send_sem, recv_sem) = rest[:6], rest[6:12], rest[12:]

    io_copies = []

    def io_copy(src, dst):
        copy = pltpu.make_async_copy(src, dst, io_sem.at[len(io_copies)])
        io_copies.append(copy)
        copy.start()
        return copy


    section = lax.axis_index("section")
    x, core = section // 2, section % 2
    y, z = lax.axis_index("replica"), lax.axis_index("dp")
    links = Links(send_sem, recv_sem)

    def x_block(dx, dz, h=None, quarter=None):
        start = (lax.rem(x + dx, NX) * NX + lax.rem(z + dz, NX)) * ROWS
        size = ROWS
        if h is not None:
            start, size = start + h * HALF, HALF
        if quarter is not None:
            start, size = start + quarter * QUARTER, QUARTER
        return x_all.at[pl.ds(pl.multiple_of(start, QUARTER), size), :]

    x_own = x_block(0, 0)
    x_in, wn_in = io_copy(x_hbm, x_own), io_copy(wn_hbm, wn_ref)

    def place(px, pc, py, pz):
        return {"section": px * 2 + pc, "replica": py, "dp": pz}

    def at(dx=0, dy=0, dz=0, flip=False):
        return place(lax.rem(x + dx, NX), 1 - core if flip else core, lax.rem(y + dy, NX), lax.rem(z + dz, NX))

    barrier = pltpu.get_barrier_semaphore()
    peers = [at(flip=True)] + [at(dx=d) for d in (1, 3, 2)] + [at(dz=d) for d in (1, 3, 2)] + [at(dy=d) for d in (1, 3, 2)]
    for peer in peers:
        pl.semaphore_signal(barrier, inc=1, device_id=peer, device_id_type=MESH)

    tile_copies = []
    for i in range(row_tiles):
        copy = pltpu.make_async_copy(
            tiles_hbm.at[pl.ds(i * slots, slots)], tile_refs[i].at[pl.ds(0, slots)], tile_sem.at[i]
        )
        copy.start()
        tile_copies.append(copy)

    cols_in, ws_in, deg_in, cot_in = (
        io_copy(cols_hbm, cols_ref), io_copy(ws_hbm, ws_ref), io_copy(deg_hbm, deg_ref), io_copy(cot_hbm, cot_ref)
    )
    x_in.wait()
    wn_in.wait()
    own = x_own[...]
    me = (x * 2 + core) * NX + z
    y_all[pl.ds(pl.multiple_of(me * ROWS, ROWS), ROWS), :] = dot(own, wn_ref[...]).astype(BF16)
    pl.semaphore_wait(barrier, len(peers))

    def block(du, dv, h=None, quarter=None):
        dx, dz = (dv, du) if h == 1 else (du, dv)
        start = ((lax.rem(x + dx, NX) * 2 + core) * NX + lax.rem(z + dz, NX)) * ROWS
        size = ROWS
        if h is not None:
            start, size = start + h * HALF, HALF
        if quarter is not None:
            start, size = start + quarter * QUARTER, QUARTER
        return y_all.at[pl.ds(pl.multiple_of(start, QUARTER), size), :]

    def along(h, d):
        return at(dx=d) if h == 0 else at(dz=d)

    def push(h, d, du, dv, quarter=None, group=None):
        ref = block(du, dv, h, quarter)
        return links.send(ref, ref, along(1 - h, d), group)

    partner = [links.group() for _ in range(NX)]

    def to_partner(dx, dz):
        ref = block(dx, dz)
        links.send(ref, ref, at(flip=True), partner[dx])

    def make_rows(i):
        tile_copies[i].wait()

        def put(q, carry):
            for k in range(8):
                c = q * 8 + k
                bands[pl.ds(i * TILE, TILE), pl.ds(pl.multiple_of(c * TILE, TILE), TILE)] = tile_refs[i][slot_ref[i, c]]
            return carry

        lax.fori_loop(0, bands.shape[1] // TILE // 8, put, 0)

    line, far = {}, {}
    rest, far_two, relay = ([links.group() for _ in range(n)] for n in (2, 2, 4))
    def send_line(h, d, part, group=None):
        ref = block(0, 0, part)
        line[h, NX - d, part] = links.send(ref, ref, along(h, d), group)

    for d in (1, 3, 2):
        for h in (0, 1):
            send_line(h, d, h)
    to_partner(0, 0)
    for d in (1, 3):
        for h in (0, 1):
            send_line(h, d, 1 - h, rest[h])

    cols_in.wait()
    shape = cols_ref.shape
    row_id = lax.broadcasted_iota(jnp.int32, shape, 0)
    count = jnp.zeros(shape, jnp.int32)
    for i in range(row_tiles):
        count = jnp.where(row_id == i, counts_ref[i], count)
    live = jnp.where(lax.broadcasted_iota(jnp.int32, shape, 1) < count, cols_ref[...], -1)
    col_id = lax.broadcasted_iota(jnp.int32, table.shape, 1)
    found = jnp.full(table.shape, slots, jnp.int32)
    for m in range(slots):
        found = jnp.where(live[:, m : m + 1] == col_id, m, found)
    table[...] = found
    table_copy = io_copy(table, slot_ref)
    for i in range(row_tiles):
        tile_refs[i][slots] = jnp.zeros((TILE, TILE), BF16)
    table_copy.wait()
    for i in range(0, 2):
        make_rows(i)

    for du in (3, 1):
        for h in (0, 1):
            line[h, du, h].wait_recv()
            far[h, du, 3] = push(h, 1, du, 0)
            far[h, du, 1] = push(h, 3, du, 0)
    for h in (0, 1):
        send_line(h, 2, 1 - h)
    ws_in.wait()
    self_pre[...] = dot(own, ws_ref[...])
    for i in range(2, 4):
        make_rows(i)
    for h in (0, 1):
        line[h, 2, h].wait_recv()
        for d in (1, 3, 2):
            push(h, d, 2, 0, group=far_two[h])
    for h in (0, 1):
        wait_all(rest[h], y_all.at[pl.ds(0, 2 * HALF), :])
        for du in (3, 1):
            to_partner(*((du, 0) if h == 0 else (0, du)))
    for i in range(4, 6):
        make_rows(i)

    def strip_of(dx, flip):
        c = 1 - core if flip else core
        return pl.ds(pl.multiple_of((lax.rem(x + dx, NX) * 2 + c) * STRIP, STRIP), STRIP)

    def spread(dx, flip, first=False):
        cols = strip_of(dx, flip)
        if flip:
            wait_all(partner[dx], y_all.at[cols, :])
        value = dot(bands[:, cols], y_all[cols, :])
        acc[...] = value if first else acc[...] + value

    for du in (3, 1):
        for dv in (3, 1):
            for h in (0, 1):
                far[h, du, dv].wait_recv()
                push(h, 1 if dv == 3 else 3, du, dv, 0 if dv == 3 else 1, relay[h + du - 1])
    for dx in (3, 1):
        for dz in (3, 1):
            to_partner(dx, dz)
    for h in (0, 1):
        line[h, 2, 1 - h].wait_recv()
        to_partner(*((2, 0) if h == 0 else (0, 2)))
    for i in range(6, 8):
        make_rows(i)
    spread(0, False, True)
    spread(0, True)
    for h in (0, 1):
        wait_all(far_two[h], y_all.at[pl.ds(0, 3 * HALF), :])
    to_partner(2, 2)
    for du in (3, 1):
        for h in (0, 1):
            wait_all(relay[h + du - 1], block(du, 2, h))
        to_partner(du, 2)
        to_partner(2, du)
    x_line, x_far = {}, {}
    x_late = links.group()

    def x_push(h, d, du, dv=0, quarter=None, group=None):
        ref = x_block(*((du, dv) if h == 0 else (dv, du)), h, quarter)
        return links.send(ref, ref, along(1 - h, d), group)

    x_rest, x_two = ([links.group() for _ in range(2)] for _ in range(2))

    def x_on(h, half, du, group):
        ref = x_block(*((du, 0) if h == 0 else (0, du)), half, 0 if du == 3 else 1)
        links.send(ref, ref, along(h, 1 if du == 3 else 3), group)

    def x_relay(du):
        for dv in (3, 1):
            for h in (0, 1):
                x_far[h, du, dv].wait_recv()
                x_push(h, 1 if dv == 3 else 3, du, dv, 0 if dv == 3 else 1, x_late)

    for d in (1, 3):
        for h in (0, 1):
            ref = x_block(0, 0, h)
            x_line[h, NX - d] = links.send(ref, ref, along(h, d))
    for d in (1, 3):
        for h in (0, 1):
            ref = x_block(0, 0, 1 - h)
            links.send(ref, ref, along(h, d), x_rest[h])
    spread(3, False)
    spread(1, False)
    spread(3, True)
    spread(1, True)
    deg_in.wait()
    cot_in.wait()
    rdeg[...] = 1.0 / jnp.broadcast_to(deg_ref[...].astype(F32), (HALF, ROWS)).T
    own_cols, flip_cols = strip_of(2, False), strip_of(2, True)
    wait_all(partner[2], y_all.at[flip_cols, :])

    def add3(a, b, c):
        return a.astype(F32) + b.astype(F32) + c.astype(F32)

    def last_rows(dy):
        rows = pl.ds(pl.multiple_of(lax.rem(y + dy, NX) * ROWS, ROWS), ROWS)
        return acc[rows, :] + dot(bands[rows, own_cols], y_all[own_cols, :]) + dot(bands[rows, flip_cols], y_all[flip_cols, :])

    parts, grads = [links.group() for _ in range(2)], [links.group() for _ in range(2)]

    def send_part(f, d):
        links.send(part_out.at[f, d - 1], part_in.at[f, d - 1], at(dy=d), parts[f])

    for d in (2, 1, 3):
        value = last_rows(d).astype(BF16)
        part_out[0, d - 1] = value[:, :HALF]
        part_out[1, d - 1] = value[:, HALF:]
        send_part(0, d)
    for d in (2, 1, 3):
        send_part(1, d)
    for du in (3, 1):
        for h in (0, 1):
            x_line[h, du].wait_recv()
            x_on(h, h, du, x_two[h])
    for du in (3, 1):
        for h in (0, 1):
            for d in (1, 3):
                x_far[h, du, NX - d] = x_push(h, d, du)
    acc[pl.ds(0, ROWS), :] = last_rows(0)
    for h in (0, 1):
        wait_all(x_rest[h], x_all.at[pl.ds(0, 2 * HALF), :])
        for du in (3, 1):
            x_on(h, 1 - h, du, x_late)
    for h in (0, 1):
        wait_all(x_two[h], x_block(*((2, 0) if h == 0 else (0, 2)), h))
        for d in (1, 3):
            x_far[h, 2, NX - d] = x_push(h, d, 2)

    own_rows = pl.ds(pl.multiple_of(y * ROWS, ROWS), ROWS)
    for f in range(2):
        cols = pl.ds(f * HALF, HALF)
        wait_all(parts[f], part_in.at[f])
        total = acc[pl.ds(0, ROWS), cols] + add3(part_in[f, 0], part_in[f, 1], part_in[f, 2])
        preact = self_pre[:, cols] + total * rdeg[...]
        sig = jax.nn.sigmoid(preact)
        slope = sig * (1.0 + preact * (1.0 - sig))
        half_pre = (cot_ref[:, cols].astype(F32) * slope).astype(BF16)
        ht[cols, own_rows] = (half_pre.astype(F32) * rdeg[...]).T.astype(BF16)
        for d in (2, 1, 3):
            links.send(ht.at[cols, own_rows], ht.at[cols, own_rows], at(dy=d), grads[f])
        pre_out[:, cols] = half_pre
        hid_ref[:, cols] = (preact * sig).astype(BF16)
    hid_out = io_copy(hid_ref, hid_hbm)
    grad_pre = pre_out[...]
    own_gf[...] = dot_nt(grad_pre, ws_ref[...])

    z_one, z_two = z + 1 - 2 * (z % 2), NX - 1 - z
    half_bit = lax.rem((z + 1) // 2, 2)

    def all_sum(value, out_ref, bufs):
        a_out, a_in, b_out, b_in, c_in, result = bufs
        depth = a_in.shape[0]
        seg = depth // 8
        mine = pl.ds(pl.multiple_of(core * depth, depth), depth)
        other = pl.ds(pl.multiple_of((1 - core) * depth, depth), depth)
        a_out[...] = value.astype(BF16)
        copy = links.send(a_out.at[other, :], a_in, at(flip=True))
        yield
        copy.wait_recv()
        b_out[...] = (a_out[mine, :].astype(F32) + a_in[...].astype(F32)).astype(BF16)

        def seg_at(d, flip_z, base=0):
            bit = 1 - half_bit if flip_z else half_bit
            return pl.ds(pl.multiple_of(base + (lax.rem(y + d, NX) * 2 + bit) * seg, seg), seg)

        group = [(2, True), (2, False), (1, True), (3, True), (1, False), (3, False), (0, True)]

        def first_peer(d, flip_z):
            return place(x, core, lax.rem(y + d, NX), z_one if flip_z else z)

        arrived = links.group()
        for n, to in enumerate(group):
            links.send(b_out.at[seg_at(*to), :], b_in.at[n], first_peer(*to), arrived)
        yield
        wait_all(arrived, b_in)
        piece = b_out[seg_at(0, False), :].astype(F32)
        for n in range(7):
            piece = piece + b_in[n].astype(F32)
        slot = x * 2 + z // 2
        c_in[slot] = piece.astype(BF16)
        arrived = links.group()
        for d, flip_z in group:
            peer = place(lax.rem(x + d, NX), core, y, z_two if flip_z else z)
            links.send(c_in.at[slot], c_in.at[slot], peer, arrived)
        yield
        wait_all(arrived, c_in.at[pl.ds(0, 7)])
        piece = c_in[0].astype(F32)
        for n in range(1, 8):
            piece = piece + c_in[n].astype(F32)
        rows = seg_at(0, False, core * depth)
        result[rows, :] = piece.astype(BF16)
        arrived = links.group()
        for to in group:
            links.send(result.at[rows, :], result.at[rows, :], first_peer(*to), arrived)
        yield
        wait_all(arrived, result.at[pl.ds(0, 7 * seg), :])
        copy = links.send(result.at[mine, :], result.at[mine, :], at(flip=True))
        yield
        copy.wait_recv()
        out_ref[...] = result[...]
        yield

    self_sum = all_sum(dot(grad_pre.astype(F32).T.astype(BF16), own), gs_ref, self_bufs)
    next(self_sum)
    next(self_sum)
    x_relay(3)
    x_relay(1)
    for f in range(2):
        wait_all(grads[f], ht.at[pl.ds(f * HALF, HALF), pl.ds(0, (NX - 1) * ROWS)])

    def collect(dx, flip):
        return dot(ht[...], bands[:, strip_of(dx, flip)])

    pair, a_lines = {}, [links.group() for _ in range(NX)]
    b_lines, a_fold, b_fold = links.group(), links.group(), links.group()
    half_a, half_b = pl.ds(0, HALF), pl.ds(HALF, HALF)

    def z_at(d):
        return lax.rem(z + d, NX)

    def give(dx):
        value = collect(dx, True).astype(BF16)
        for k in range(NX):
            pair_out[dx, k] = value[:, k * ROWS : (k + 1) * ROWS]
        pair[dx] = links.send(pair_out.at[dx], pair_in.at[dx], at(flip=True))

    def keep(dx):
        value = collect(dx, False)
        pair[dx].wait_recv()
        for k in range(NX):
            sums[dx, k] = (value[:, k * ROWS : (k + 1) * ROWS] + pair_in[dx, k].astype(F32)).astype(BF16)
        for d in (2, 1, 3):
            links.send(sums.at[dx, z_at(d), half_a], az.at[dx, d - 1], at(dz=d), a_lines[dx])
        if dx:
            links.send(sums.at[dx, :, half_b], bx.at[dx - 1], at(dx=dx), b_lines)

    def a_close(dx):
        wait_all(a_lines[dx], az.at[dx])
        total = sums[dx, z, half_a].astype(F32) + add3(az[dx, 0], az[dx, 1], az[dx, 2])
        mid_a[dx] = total.astype(BF16)
        if dx:
            links.send(mid_a.at[dx], ax.at[dx - 1], at(dx=dx), a_fold)

    def b_close(dz):
        total = sums[0, z_at(dz), half_b].astype(F32) + add3(bx[0, z_at(dz)], bx[1, z_at(dz)], bx[2, z_at(dz)])
        mid_b[dz] = total.astype(BF16)
        if dz:
            links.send(mid_b.at[dz], bz.at[dz - 1], at(dz=dz), b_fold)

    give(2)
    give(1)
    x_relay(2)
    keep(2)
    give(3)
    keep(1)
    give(0)
    keep(3)
    keep(0)

    wait_all(x_late, x_all.at[pl.ds(0, 16 * QUARTER), :])

    def x_strip(dx):
        return x_all[pl.ds(pl.multiple_of(lax.rem(x + dx, NX) * STRIP, STRIP), STRIP), :]

    term = dot(jnp.concatenate([sums[0, k] for k in range(NX)], axis=1), x_strip(0))
    for dx in range(1, NX):
        term = term + dot(jnp.concatenate([sums[dx, k] for k in range(NX)], axis=1), x_strip(dx))
    neigh_sum = all_sum(term, gn_ref, neigh_bufs)
    next(neigh_sum)
    next(self_sum)
    next(neigh_sum)
    a_close(2)
    a_close(1)
    next(neigh_sum)
    a_close(3)
    wait_all(b_lines, bx)
    for d in (2, 1, 3, 0):
        b_close(d)
    a_close(0)
    next(self_sum)
    next(neigh_sum)
    wait_all(a_fold, ax)
    wait_all(b_fold, bz)
    sum_a = mid_a[0].astype(F32) + add3(ax[0], ax[1], ax[2])
    sum_b = mid_b[0].astype(F32) + add3(bz[0], bz[1], bz[2])
    back = jnp.concatenate([sum_a, sum_b], axis=0).T.astype(BF16)
    gf_ref[...] = (own_gf[...] + dot_nt(back, wn_ref[...])).astype(BF16)
    gf_out = io_copy(gf_ref, gf_hbm)
    for _ in self_sum:
        pass
    gs_out = io_copy(gs_ref, gs_hbm)
    for _ in neigh_sum:
        pass
    gn_out = io_copy(gn_ref, gn_hbm)
    links.drain()
    for copy in (hid_out, gf_out, gs_out, gn_out):
        copy.wait()


def finish(node_scale, hid_in, gf_in, gs_in, gn_in, hid_ref, gf_ref, gs_ref, gn_ref):
    hid_ref[...] = hid_in[...]
    gf_ref[...] = gf_in[...]
    gs_ref[...] = gs_in[...].astype(F32).T * node_scale
    gn_ref[...] = gn_in[...].astype(F32).T * node_scale


def local(features, tile_vals, tile_cols, row_counts, degrees, w_self, w_neigh, cotangent):
    f_in, f_out = w_self.shape
    _, _, row_tiles, slots = tile_cols.shape
    col_tiles = lax.axis_size(("section", "dp")) * ROWS // TILE
    nodes = lax.axis_size(("section", "replica", "dp")) * ROWS

    def vmem(*shape, dtype=BF16):
        return pltpu.VMEM(shape, dtype)

    def sum_buffers():
        depth = f_out // 2
        return [
            vmem(f_out, f_in), vmem(depth, f_in), vmem(depth, f_in), vmem(7, depth // 8, f_in),
            vmem(8, depth // 8, f_in), vmem(f_out, f_in),
        ]

    scratch = [vmem(slots + 1, TILE, TILE) for _ in range(row_tiles)] + [
        vmem(row_tiles, 128, dtype=jnp.int32),
        pltpu.SMEM((row_tiles, 128), jnp.int32),
        vmem(row_tiles * TILE, col_tiles * TILE),
        vmem(col_tiles * TILE, f_out),
        vmem(row_tiles * TILE, f_out, dtype=F32),
        vmem(ROWS, f_out, dtype=F32),
        vmem(ROWS, HALF, dtype=F32),
        vmem(2, NX - 1, ROWS, HALF),
        vmem(2, NX - 1, ROWS, HALF),
        vmem(ROWS, f_out),
        vmem(f_out, NX * ROWS),
        vmem(NX, NX, f_out, ROWS),
        vmem(NX, NX, f_out, ROWS),
        vmem(NX, NX, f_out, ROWS),
        vmem(NX, NX - 1, HALF, ROWS),
        vmem(NX - 1, NX, HALF, ROWS),
        vmem(NX, HALF, ROWS),
        vmem(NX, HALF, ROWS),
        vmem(NX - 1, HALF, ROWS),
        vmem(NX - 1, HALF, ROWS),
        vmem(NX * STRIP, f_in),
        vmem(ROWS, f_in, dtype=F32),
        vmem(row_tiles, slots, dtype=jnp.int32),
        vmem(1, ROWS, dtype=jnp.int32),
        vmem(f_in, f_out),
        vmem(f_in, f_out),
        vmem(ROWS, f_out),
        vmem(ROWS, f_out),
        vmem(ROWS, f_in),
        vmem(f_out, f_in),
        vmem(f_out, f_in),
        *sum_buffers(),
        *sum_buffers(),
        pltpu.SemaphoreType.DMA((row_tiles,)),
        pltpu.SemaphoreType.DMA((16,)),
        pltpu.SemaphoreType.DMA((N_SEND,)),
        pltpu.SemaphoreType.DMA((N_RECV,)),
    ]
    in_vmem = pl.BlockSpec(memory_space=pltpu.VMEM)
    in_smem = pl.BlockSpec(memory_space=pltpu.SMEM)
    in_any = pl.BlockSpec(memory_space=pl.ANY)
    raw = pl.pallas_call(
        kernel,
        out_shape=(
            jax.ShapeDtypeStruct((ROWS, f_out), BF16),
            jax.ShapeDtypeStruct((ROWS, f_in), BF16),
            jax.ShapeDtypeStruct((f_out, f_in), BF16),
            jax.ShapeDtypeStruct((f_out, f_in), BF16),
        ),
        in_specs=[in_any, in_any, in_any, in_smem, in_any, in_any, in_any, in_any],
        out_specs=(in_any,) * 4,
        scratch_shapes=scratch,
        compiler_params=pltpu.CompilerParams(
            collective_id=0, has_side_effects=True, vmem_limit_bytes=58 * 1024 * 1024
        ),
        name="sage_layer",
    )(
        features[0],
        tile_vals.reshape(row_tiles * slots, TILE, TILE),
        tile_cols[0, 0],
        row_counts[0, 0],
        degrees,
        w_self,
        w_neigh,
        cotangent[0],
    )
    hidden, grad_features, grad_self, grad_neigh = pl.pallas_call(
        functools.partial(finish, 1.0 / math.sqrt(nodes)),
        out_shape=(
            jax.ShapeDtypeStruct((ROWS, f_out), BF16),
            jax.ShapeDtypeStruct((ROWS, f_in), BF16),
            jax.ShapeDtypeStruct((f_in, f_out), F32),
            jax.ShapeDtypeStruct((f_in, f_out), F32),
        ),
        in_specs=[in_vmem] * 4,
        out_specs=(in_vmem,) * 4,
        name="finish",
    )(*raw)
    return hidden[None], grad_features[None], grad_self, grad_neigh


def solution(mesh):
    node = P(("section", "dp"), "replica", None)
    placed = (
        node,
        P(("section", "dp"), "replica", None, None, None, None),
        P(("section", "dp"), "replica", None, None),
        P(("section", "dp"), "replica", None),
        P(("section", "dp"), "replica"),
        P(),
        P(),
        node,
    )
    return jax.shard_map(local, mesh=mesh, in_specs=placed, out_specs=(node, node, P(), P()), check_vma=False)
```
